512 devices in a mesh: section: 32 (over x_hi, z, core), rep: 16 (over y, x_lo).
Axes of the slice: x: 4 (x_hi: 2, x_lo: 2; x = x_hi * 2 + x_lo), y: 8, z: 8, core: 2. Of those that a mesh axis runs over, the one named last changes fastest.
Arguments:
- features: bfloat16 [65536, 256], P(('section', 'rep')), may hold values from -6 to 6
- weight: bfloat16 [256, 256], replicated, may hold values from -0.375 to 0.375
- cotangent: bfloat16 [65536, 256], P(('section', 'rep')), may hold values from -6 to 6
- tile_values: bfloat16 [32, 16, 32, 2, 128, 128], P('section', 'rep'), may hold values from -0.09375 to 0.09375
- tile_cols: int32 [32, 16, 32, 2], P('section', 'rep'), may hold values from 0 to 15
- tile_counts: int32 [32, 16, 32], P('section', 'rep'), may hold values from 0 to 2, as said below
Outputs:
- output: bfloat16 [65536, 256], P(('section', 'rep'))
- grad_features: bfloat16 [65536, 256], P(('section', 'rep'))
- grad_weight: float32 [256, 256], replicated
The draws below stay inside these ranges and needn't reach their ends.
Inputs may be any that keep to these rules, and one draw needn't show every extreme that they name: `tile_cols`: column tile of each slot inside the column section's block of 16 tiles; slots at or past the count are unused. `tile_counts`: live slots of each list; every row block has one column section whose list holds 2 live tiles.
All inputs are finite; a program needn't handle non-finite values.
Results may differ from the reference program's by a relative error of at most 0.023.
Values may be sent and summed in bfloat16 or wider, within the bound.
A program may use at most 64 MiB of HBM per device.

```python
import math
import jax
import jax.numpy as jnp
from jax import lax

D = 256
TILE = 128
SLOTS = 2
SECTIONS = 32
REPS = 16
NODES = 65536


def draw_tile_counts(key, part):
    key = jax.random.fold_in(key, 11)
    key_load, key_base, key_extra, key_full = jax.random.split(key, 4)
    load = jax.random.randint(key_load, (1, 1, SECTIONS), 0, SLOTS + 1)
    base = jax.random.randint(key_base, (SECTIONS, REPS, SECTIONS), 0, 1 << 20) % (load + 1)
    extra = jax.random.randint(key_extra, (SECTIONS, REPS, SECTIONS), 0, 2)
    full_section = jax.random.randint(key_full, (SECTIONS, REPS, 1), 0, SECTIONS)
    full = jnp.arange(SECTIONS)[None, None, :] == full_section
    counts = jnp.minimum(base + extra, SLOTS)
    return jnp.where(full, SLOTS, counts).astype(jnp.int32)


def plant(values, rng, low, high):
    longest = values.shape.index(max(values.shape))
    spots = []
    for shift in (0, 1):
        where = [jax.random.randint(jax.random.fold_in(rng, axis), (), 0, length) for axis, length in enumerate(values.shape)]
        where[longest] = (where[longest] + shift) % values.shape[longest]
        spots.append(tuple(where))
    return values.at[spots[0]].set(low).at[spots[1]].set(high)


def shard_levels(stream_key, dims, cuts, low, top_value):
    gain, own = 1.0, jax.random.fold_in(stream_key, 6)
    for dim, blocks in cuts:
        draws = jnp.exp(jax.random.uniform(jax.random.fold_in(own, dim), (blocks,), jnp.float32, low / len(cuts), top_value / len(cuts)))
        gain = gain * jnp.repeat(draws, dims[dim] // blocks).reshape([-1 if axis == dim else 1 for axis in range(len(dims))])
    return gain


def normal_values(own_key, extent, scale, limit, cuts=(), dtype=jnp.bfloat16):
    values = scale * jax.random.normal(own_key, extent, jnp.float32)
    if cuts:
        values = values * shard_levels(own_key, extent, cuts, -0.22, 0.18)
    return jnp.clip(values, -limit, limit).astype(dtype)


def setup_inputs(seed: int = 0) -> dict:
    keys = jax.random.split(jax.random.key(seed), 7)
    features = normal_values(keys[0], (NODES, D), 1.0, 6.0, ((0, 512),))
    weight = normal_values(keys[1], (D, D), D ** -0.5, 0.375)
    cotangent = normal_values(keys[2], (NODES, D), 1.0, 6.0, ((0, 512),))
    tile_values = normal_values(keys[3], (SECTIONS, REPS, SECTIONS, SLOTS, TILE, TILE), (TILE * SECTIONS * SLOTS // 2) ** -0.5, 0.09375, ((0, 32), (1, 16)))
    tile_cols = plant(jax.random.randint(keys[4], (SECTIONS, REPS, SECTIONS, SLOTS), 0, REPS), jax.random.fold_in(keys[4], 1), 0, REPS - 1).astype(jnp.int32)
    tile_counts = draw_tile_counts(jax.random.fold_in(keys[6], 71), 0)
    return dict(features=features, weight=weight, cotangent=cotangent, tile_values=tile_values, tile_cols=tile_cols, tile_counts=tile_counts)


def reference(features, weight, cotangent, tile_values, tile_cols, tile_counts):
    x_tiles = features.reshape(SECTIONS, REPS, TILE, D)
    live = jnp.arange(SLOTS)[None, None, None, :] < tile_counts[..., None]
    blocks = SECTIONS * REPS
    all_tiles = tile_values.reshape(blocks, SECTIONS, SLOTS, TILE, TILE)
    all_cols = tile_cols.reshape(blocks, SECTIONS, SLOTS).astype(jnp.int32)
    all_live = live.reshape(blocks, SECTIONS, SLOTS)
    section_ids = jnp.arange(SECTIONS).astype(jnp.int32)[:, None]

    def forward_block(pieces):
        tiles, cols, mask = pieces
        chosen = x_tiles[section_ids, cols].astype(jnp.float32)
        masked = tiles.astype(jnp.float32) * mask[..., None, None].astype(jnp.float32)
        return jnp.einsum('cskj,csjd->kd', masked, chosen)
    summed = lax.map(forward_block, (all_tiles, all_cols, all_live))
    aggregated = summed.reshape(NODES, D).astype(jnp.bfloat16)
    pre = jnp.dot(aggregated, weight, preferred_element_type=jnp.float32)
    output = jax.nn.silu(pre).astype(jnp.bfloat16)
    sig = jax.nn.sigmoid(pre)
    grad_pre = (cotangent.astype(jnp.float32) * sig * (1.0 + pre * (1.0 - sig))).astype(jnp.bfloat16)
    grad_weight = jnp.dot(aggregated.T, grad_pre, preferred_element_type=jnp.float32) / math.sqrt(NODES)
    grad_aggr = jnp.dot(grad_pre, weight.T, preferred_element_type=jnp.float32).astype(jnp.bfloat16)
    g_blocks = grad_aggr.reshape(blocks, TILE, D)

    def backward_block(total, pieces):
        tiles, cols, mask, grads = pieces
        masked = tiles.astype(jnp.float32) * mask[..., None, None].astype(jnp.float32)
        contrib = jnp.einsum('cskj,kd->csjd', masked, grads.astype(jnp.float32))
        return (total.at[section_ids, cols].add(contrib), None)
    start = jnp.zeros((SECTIONS, REPS, TILE, D), jnp.float32)
    total, unused = lax.scan(backward_block, start, (all_tiles, all_cols, all_live, g_blocks))
    grad_features = total.reshape(NODES, D).astype(jnp.bfloat16)
    return (output, grad_features, grad_weight)
```

```python
import jax
import jax.numpy as jnp
from jax import lax
from jax.experimental import pallas as pl
from jax.experimental.pallas import tpu as pltpu
from jax.sharding import PartitionSpec as P

MESH = pl.DeviceIdType.MESH
F32 = jnp.float32
BF16 = jnp.bfloat16
NX, NY, NZ = 4, 8, 8
ZH = NZ // 2
GROUP = 8
SLOTS = 2
TILE = 128
D = 256
TERMS = ZH * GROUP * SLOTS
ZERO = TERMS


def device(x, y, z, k):
    return ((x // 2) * (2 * NZ) + z * 2 + k, y * 2 + x % 2)


def kernel(
    feat_ref, weight_ref, cot_ref, cols_ref, counts_ref, tiles_ref,
    out_ref, gf_ref, gw_ref,
    tiles_rx, meta_tx, meta_rx, meta_sm, prev_sm, last_sm,
    feats, part_tx, part_rx, grad_tx, grad_rx, chain,
    sib_tx, sib_rx, up_tx, up_rx, down_tx, down_rx, own_tx, own_rx,
    gw1_tx, gw1_rx, gw2_tx, gw2_rx, gw3_rx, gw4_rx, gw5_rx,
    local_sem, tile_s, tile_r, meta_s, meta_r, gat_s, gat_r,
    up_s, up_r, down_s, down_r, agd_s, agd_r, part_s, part_r, grad_s, grad_r,
    sib_s, sib_r, ups_s, ups_r, downs_s, downs_r, own_s, own_r,
    gw_s, gw_r,
):
    section, rep = lax.axis_index("section"), lax.axis_index("rep")
    xh, z, k = section // (2 * NZ), (section // 2) % NZ, section % 2
    y, xl = rep // 2, rep % 2
    x = 2 * xh + xl
    yh, yp, zh, zp = y // 2, y % 2, z // 2, z % 2
    member = x * 2 + k
    turn = 1 - 2 * k
    xpair = (x + turn * (1 - 2 * xl) + NX) % NX
    ypair = (y + turn * (1 - 2 * yp) + NY) % NY
    zpair = (z + turn * (1 - 2 * zp) + NZ) % NZ
    mine = xl * 4 + yp * 2 + zp
    sibling = device(x, y, z, 1 - k)
    alone = jnp.logical_and(xl == k, xh == yp)
    away = jnp.logical_not(alone)

    def swap(core, a, b):
        return a + core * (b - a), b - core * (b - a)

    u0, v0 = swap(k, yh, zh)
    uh, vh = swap(xl, yh, zh)
    vs = [(v0 + i) % ZH for i in range(ZH)]

    def gatherer(i, a):
        yy, zz = swap(xl, uh, (vh + i) % ZH)
        return device(2 * ((xh + a) % 2) + k, 2 * yy + xh, 2 * zz + zp, xl)

    def owner(i, e):
        yy, zz = swap(k, u0, vs[i])
        return device(2 * yp + k, 2 * yy + (yp + e) % 2, 2 * zz + zp, xl)

    def along(j):
        yy, zz = swap(k, (u0 + j + ZH) % ZH, v0)
        return device(x, 2 * yy + yp, 2 * zz + zp, k)

    def group(o):
        px, py, pz = (xl + o // 4) % 2, (yp + (o // 2) % 2) % 2, (zp + o % 2) % 2
        return px, py, pz, px * 4 + py * 2 + pz

    def peer(o):
        px, py, pz, p = group(o)
        dev = device(xpair if o & 4 else x, ypair if o & 2 else y, zpair if o & 1 else z, k)
        return (py, pz, px), p, dev

    def copy(src, dst, send, recv, dev):
        return pltpu.make_async_remote_copy(
            src_ref=src, dst_ref=dst, send_sem=send, recv_sem=recv,
            device_id=dev, device_id_type=MESH,
        )

    sent = []

    def send(src, dst, ssem, rsem, dev):
        c = copy(src, dst, ssem, rsem, dev)
        c.start()
        sent.append(c)

    def arrived(dst, ssem, rsem):
        copy(dst, dst, ssem, rsem, sibling).wait_recv()

    ypeers = [(y + i) % NY for i in range(1, NY)]
    zpeers = [(z + i) % NZ for i in range(1, NZ)]
    mpeers = [(member + i) % GROUP for i in range(1, GROUP)]

    own_tiles = pltpu.make_async_copy(
        tiles_ref.at[yp, :, zp, xl], tiles_rx.at[mine], local_sem.at[0]
    )
    own_tiles.start()

    barrier = pltpu.get_barrier_semaphore()
    everyone = (
        [device(x, j, z, k) for j in ypeers]
        + [device(x, y, j, k) for j in zpeers]
        + [device(j // 2, y, z, j % 2) for j in mpeers]
        + [peer(o)[2] for o in (3, 5, 6, 7)]
        + [f(i, a) for f in (gatherer, owner) for i in range(ZH) for a in range(2) if i or a]
    )
    for dev in everyone:
        pl.semaphore_signal(barrier, inc=1, device_id=dev, device_id_type=MESH)

    @pl.when(away)
    def _():
        for dev in (gatherer(0, 0), owner(0, 0)):
            pl.semaphore_signal(barrier, inc=1, device_id=dev, device_id_type=MESH)

    pl.semaphore_wait(barrier, len(everyone) + jnp.where(away, 2, 0))

    own_slot = feats.at[xl, uh, vh, yp]

    @pl.when(alone)
    def _():
        feats[xl, uh, vh, yp] = feat_ref[...]

    @pl.when(away)
    def _():
        copy(feat_ref, own_slot, gat_s.at[0, 0], gat_r.at[vh, yp], gatherer(0, 0)).start()

    for i in range(ZH):
        for a in range(2):
            if i or a:
                send(feat_ref, own_slot, gat_s.at[i, a], gat_r.at[vh, yp], gatherer(i, a))

    dead = lax.broadcasted_iota(jnp.int32, (SLOTS, 32), 0) >= counts_ref[...]
    meta_tx[...] = jnp.zeros_like(meta_tx)
    meta_tx[0:SLOTS, 0:32] = cols_ref[...] + jnp.where(dead, 2 * NY, 0)
    for o in range(1, GROUP):
        which, p, dev = peer(o)
        send(meta_tx, meta_rx.at[mine], meta_s.at[o], meta_r.at[mine], dev)
    for o in range(1, GROUP):
        (ch, cz, ck), p, dev = peer(o)
        send(tiles_ref.at[ch, :, cz, ck], tiles_rx.at[mine], tile_s.at[o], tile_r.at[mine], dev)
    meta_rx[mine] = meta_tx[...]

    up, down = along(1), along(-1)

    def uu(j):
        return (u0 + j + ZH) % ZH

    def gather_up(s, i):
        part = feats.at[k, uu(-s), vs[i]]
        send(part, part, up_s.at[s, i], up_r.at[s, i], up)

    def gather_down(s, i):
        part = feats.at[k, uu(s), vs[i]]
        send(part, part, down_s.at[s, i], down_r.at[s, i], down)

    def gather_sibling(j):
        part = feats.at[k, uu(j)]
        send(part, part, agd_s.at[j], agd_r.at[uu(j)], sibling)

    for i in range(ZH):
        arrived(feats.at[k, u0, vs[i], 1 - yp], gat_s.at[i, 1], gat_r.at[vs[i], 1 - yp])
        if i == 0:
            @pl.when(away)
            def _():
                arrived(feats.at[k, u0, v0, yp], gat_s.at[0, 0], gat_r.at[v0, yp])
        else:
            arrived(feats.at[k, u0, vs[i], yp], gat_s.at[i, 0], gat_r.at[vs[i], yp])
        gather_up(0, i)
        gather_down(0, i)
    gather_sibling(0)
    for i in (0, 2, 1, 3):
        arrived(feats.at[k, uu(-1), vs[i]], up_s.at[0, i], up_r.at[0, i])
        if i < 2:
            gather_up(1, i)
        arrived(feats.at[k, uu(1), vs[i]], down_s.at[0, i], down_r.at[0, i])
        if i >= 2:
            gather_down(1, i)
    gather_sibling(1)
    gather_sibling(3)
    for i in (0, 1):
        arrived(feats.at[k, uu(2), vs[i]], up_s.at[1, i], up_r.at[1, i])
        arrived(feats.at[k, uu(2), vs[i + 2]], down_s.at[1, i + 2], down_r.at[1, i + 2])
    gather_sibling(2)

    for o in range(1, GROUP):
        p = peer(o)[1]
        arrived(meta_rx.at[p], meta_s.at[o], meta_r.at[p])
    to_scalar = pltpu.make_async_copy(meta_rx, meta_sm, local_sem.at[1])
    to_scalar.start()
    to_scalar.wait()

    def column_section(c):
        return yp * (2 * NZ) + c * 4 + zp * 2 + xl

    @pl.loop(0, ZH * 2 * NY)
    def _(q):
        last_sm[q] = ZERO

    @pl.loop(0, TERMS)
    def _(i):
        c, o, s = i // (GROUP * SLOTS), (i // SLOTS) % GROUP, i % SLOTS
        col = meta_sm[group(o)[3], s, column_section(c)] % (2 * NY)
        prev_sm[i] = last_sm[c * 2 * NY + col]
        for q in range(2 * NY):
            last_sm[c * 2 * NY + q] = jnp.where(col == q, i, last_sm[c * 2 * NY + q])

    chain[ZERO] = jnp.zeros((D, TILE), F32)

    for c in range(ZH):
        arrived(feats.at[1 - k, c], agd_s.at[c], agd_r.at[c])

    def live_tiles(p, c):
        tiles, codes = [], []
        for s in range(SLOTS):
            code = meta_sm[p, s, column_section(c)]
            tile = tiles_rx[p, c, s]
            tiles.append(jnp.where(code < 2 * NY, tile, jnp.zeros_like(tile)))
            codes.append(code % (2 * NY))
        return jnp.concatenate(tiles, axis=1), codes

    total = None
    for o in (1, 2, 4, 3, 5, 6, 7, 0):
        which, p, dev = peer(o)
        if o == 0:
            own_tiles.wait()
        else:
            arrived(tiles_rx.at[p], tile_s.at[o], tile_r.at[p])
        acc = jnp.zeros((TILE, D), F32)
        for c in range(ZH):
            pair, cols = live_tiles(p, c)
            rows = []
            for col in cols:
                u, v = swap(col % 2, col // 4, c)
                rows.append(feats[col % 2, u, v, (col // 2) % 2])
            rows = jnp.concatenate(rows, axis=0)
            acc += jnp.dot(pair, rows, preferred_element_type=F32)
        if o == 0:
            total = acc
        else:
            part_tx[o] = acc.astype(BF16)
            send(part_tx.at[o], part_rx.at[mine], part_s.at[o], part_r.at[mine], dev)
    for o in range(1, GROUP):
        p = peer(o)[1]
        arrived(part_rx.at[p], part_s.at[o], part_r.at[p])
        total += part_rx[p].astype(F32)

    aggregated = total.astype(BF16)
    weight = weight_ref[...]
    pre = jnp.dot(aggregated, weight, preferred_element_type=F32)
    sig = lax.logistic(pre)
    out_ref[...] = (pre * sig).astype(BF16)
    grad_pre = (cot_ref[...].astype(F32) * sig * (1.0 + pre * (1.0 - sig))).astype(BF16)
    grad_tx[...] = lax.dot_general(
        weight, grad_pre, (((1,), (1,)), ((), ())), preferred_element_type=F32
    ).astype(BF16)
    for o in range(1, GROUP):
        which, p, dev = peer(o)
        send(grad_tx, grad_rx.at[mine], grad_s.at[o], grad_r.at[mine], dev)

    terms = lax.dot_general(
        aggregated, grad_pre, (((0,), (0,)), ((), ())), preferred_element_type=F32
    )
    for i in range(NZ):
        for j in range(GROUP):
            r0, c0 = i * 32 + (j % 4) * 8, (j // 4) * 128
            gw1_tx[i, j] = terms[r0:r0 + 8, c0:c0 + 128]
    for i, j in enumerate(zpeers):
        send(gw1_tx.at[j], gw1_rx.at[z], gw_s.at[0, i], gw_r.at[0, z], device(x, y, j, k))
    gw1_rx[z] = gw1_tx[z]

    for o in range(GROUP):
        which, p, dev = peer(o)
        if o == 0:
            grads = grad_tx[...]
        else:
            arrived(grad_rx.at[p], grad_s.at[o], grad_r.at[p])
            grads = grad_rx[p]
        for c in range(ZH):
            pair, cols = live_tiles(p, c)
            both = jnp.dot(grads, pair, preferred_element_type=F32)
            for s in range(SLOTS):
                i = c * GROUP * SLOTS + o * SLOTS + s
                chain[i] = both[:, s * TILE:(s + 1) * TILE] + chain[prev_sm[i]]

    for i, j in enumerate(zpeers):
        arrived(gw1_rx.at[j], gw_s.at[0, i], gw_r.at[0, j])
    gw2_tx[...] = jnp.sum(gw1_rx[...], axis=0)
    for i, j in enumerate(mpeers):
        send(gw2_tx.at[j], gw2_rx.at[member], gw_s.at[1, i], gw_r.at[1, member], device(j // 2, y, z, j % 2))
    gw2_rx[member] = gw2_tx[member]

    def block(half, u, v, e):
        yy, c = swap(half, u, v)
        return chain[last_sm[c * 2 * NY + (2 * yy + e) * 2 + half]]

    for j in (2, 1, 3, 0):
        u = (v0 + j) % ZH
        for v in range(ZH):
            for e in range(2):
                sib_tx[u, v, e] = block(1 - k, u, v, e).astype(BF16)
        send(sib_tx.at[u], sib_rx.at[u], sib_s.at[j], sib_r.at[u], sibling)

    for i, j in enumerate(mpeers):
        arrived(gw2_rx.at[j], gw_s.at[1, i], gw_r.at[1, j])
    gw3_rx[y] = jnp.sum(gw2_rx[...], axis=0)
    for i, j in enumerate(ypeers):
        send(gw3_rx.at[y], gw3_rx.at[y], gw_s.at[2, i], gw_r.at[2, y], device(x, j, z, k))

    def both_cores(u, v, e):
        return block(k, u, v, e) + sib_rx[u, v, e].astype(F32)

    def sibling_arrived(u):
        arrived(sib_rx.at[u], sib_s.at[0], sib_r.at[u])

    def reduce_step(u, i, slot, before, tx, rx, ssem, rsem, dev):
        if before is not None:
            arrived(rx.at[before], ssem.at[before], rsem.at[before])
        for e in range(2):
            value = both_cores(u, vs[i], e)
            if before is not None:
                value += rx[before, e].astype(F32)
            tx[slot, e] = value.astype(BF16)
        send(tx.at[slot], rx.at[slot], ssem.at[slot], rsem.at[slot], dev)

    ups = (up_tx, up_rx, ups_s, ups_r, up)
    downs = (down_tx, down_rx, downs_s, downs_r, down)
    sibling_arrived(uu(2))
    for i in range(2):
        reduce_step(uu(2), i, i, None, *ups)
        reduce_step(uu(2), i + 2, i, None, *downs)
    sibling_arrived(uu(1))
    sibling_arrived(uu(-1))
    for i in range(2):
        reduce_step(uu(1), i + 2, i + 4, None, *ups)
        reduce_step(uu(-1), i, i + 2, None, *downs)

    for i, j in enumerate(ypeers):
        arrived(gw3_rx.at[j], gw_s.at[2, i], gw_r.at[2, j])
    gw4_rx[member] = jnp.sum(gw3_rx[...], axis=0)
    for i, j in enumerate(mpeers):
        send(gw4_rx.at[member], gw4_rx.at[member], gw_s.at[3, i], gw_r.at[3, member], device(j // 2, y, z, j % 2))

    for i in range(2):
        reduce_step(uu(1), i, i + 2, i, *ups)
        reduce_step(uu(-1), i + 2, i + 4, i, *downs)

    for i, j in enumerate(mpeers):
        arrived(gw4_rx.at[j], gw_s.at[3, i], gw_r.at[3, j])
    gw5_rx[z] = gw4_rx[...]
    for i, j in enumerate(zpeers):
        send(gw5_rx.at[z], gw5_rx.at[z], gw_s.at[4, i], gw_r.at[4, z], device(x, y, j, k))

    sibling_arrived(u0)
    for i in (2, 3, 1, 0):
        arrived(up_rx.at[i + 2], ups_s.at[i + 2], ups_r.at[i + 2])
        arrived(down_rx.at[i + 2], downs_s.at[i + 2], downs_r.at[i + 2])
        for a in (1, 0):
            e = (yp + a) % 2
            value = both_cores(u0, vs[i], e) + up_rx[i + 2, e].astype(F32) + down_rx[i + 2, e].astype(F32)
            own_tx[i, a] = value.astype(BF16)
            if i or a:
                send(own_tx.at[i, a], own_rx.at[v0, xh], own_s.at[i, a], own_r.at[v0, xh], owner(i, a))

    @pl.when(alone)
    def _():
        own_rx[v0, xh] = own_tx[0, 0]

    @pl.when(away)
    def _():
        copy(own_tx.at[0, 0], own_rx.at[v0, xh], own_s.at[0, 0], own_r.at[v0, xh], owner(0, 0)).start()

    for i, j in enumerate(zpeers):
        arrived(gw5_rx.at[j], gw_s.at[4, i], gw_r.at[4, j])
    scale = 1.0 / 256.0
    for i in range(NZ):
        for j in range(GROUP):
            r0, c0 = i * 32 + (j % 4) * 8, (j // 4) * 128
            gw_ref[r0:r0 + 8, c0:c0 + 128] = gw5_rx[i, j] * scale

    for i in range(ZH):
        for a in range(2):
            v, h = (vh + i) % ZH, (xh + a) % 2
            if i or a:
                arrived(own_rx.at[v, h], own_s.at[i, a], own_r.at[v, h])

    @pl.when(away)
    def _():
        arrived(own_rx.at[vh, xh], own_s.at[0, 0], own_r.at[vh, xh])

    gf_ref[...] = jnp.sum(own_rx[...].astype(F32), axis=(0, 1)).T.astype(BF16)

    @pl.when(away)
    def _():
        copy(own_tx.at[0, 0], own_rx.at[v0, xh], own_s.at[0, 0], own_r.at[v0, xh], owner(0, 0)).wait_send()
        copy(feat_ref, own_slot, gat_s.at[0, 0], gat_r.at[vh, yp], gatherer(0, 0)).wait_send()

    for c in sent:
        c.wait_send()


def finish(out_in, gf_in, gw_in, out_ref, gf_ref, gw_ref):
    out_ref[...] = out_in[...]
    gf_ref[...] = gf_in[...]
    gw_ref[...] = gw_in[...]


def body(features, weight, cotangent, tile_values, tile_cols, tile_counts):
    cols = tile_cols.reshape(32, SLOTS).T
    counts = tile_counts.reshape(1, 32)
    tiles = tile_values.reshape(2, ZH, 2, 2, SLOTS, TILE, TILE)
    dma, vmem = pltpu.SemaphoreType.DMA, pltpu.VMEM
    spec = pl.BlockSpec(memory_space=pltpu.VMEM)
    block = (D, TILE)
    results = pl.pallas_call(
        kernel,
        out_shape=(
            jax.ShapeDtypeStruct((TILE, D), BF16),
            jax.ShapeDtypeStruct((TILE, D), BF16),
            jax.ShapeDtypeStruct((D, D), F32),
        ),
        in_specs=[spec] * 5 + [pl.BlockSpec(memory_space=pl.ANY)],
        out_specs=(spec,) * 3,
        scratch_shapes=[
            vmem((GROUP, ZH, SLOTS, TILE, TILE), BF16),
            vmem((8, 128), jnp.int32),
            vmem((GROUP, 8, 128), jnp.int32),
            pltpu.SMEM((GROUP, 8, 128), jnp.int32),
            pltpu.SMEM((TERMS,), jnp.int32),
            pltpu.SMEM((ZH * 2 * NY,), jnp.int32),
            vmem((2, ZH, ZH, 2, TILE, D), BF16),
            vmem((GROUP, TILE, D), BF16),
            vmem((GROUP, TILE, D), BF16),
            vmem(block, BF16),
            vmem((GROUP,) + block, BF16),
            vmem((TERMS + 1,) + block, F32),
            vmem((ZH, ZH, 2) + block, BF16),
            vmem((ZH, ZH, 2) + block, BF16),
            vmem((6, 2) + block, BF16),
            vmem((6, 2) + block, BF16),
            vmem((6, 2) + block, BF16),
            vmem((6, 2) + block, BF16),
            vmem((ZH, 2) + block, BF16),
            vmem((ZH, 2) + block, BF16),
            vmem((NZ, GROUP, 8, 128), F32),
            vmem((NZ, GROUP, 8, 128), F32),
            vmem((GROUP, 8, 128), F32),
            vmem((GROUP, 8, 128), F32),
            vmem((NY, 8, 128), F32),
            vmem((GROUP, 8, 128), F32),
            vmem((NZ, GROUP, 8, 128), F32),
            dma((2,)),
            dma((GROUP,)), dma((GROUP,)),
            dma((GROUP,)), dma((GROUP,)),
            dma((ZH, 2)), dma((ZH, 2)),
            dma((2, ZH)), dma((2, ZH)),
            dma((2, ZH)), dma((2, ZH)),
            dma((ZH,)), dma((ZH,)),
            dma((GROUP,)), dma((GROUP,)),
            dma((GROUP,)), dma((GROUP,)),
            dma((ZH,)), dma((ZH,)),
            dma((6,)), dma((6,)),
            dma((6,)), dma((6,)),
            dma((ZH, 2)), dma((ZH, 2)),
            dma((5, 8)), dma((5, 8)),
        ],
        compiler_params=pltpu.CompilerParams(
            collective_id=0, has_side_effects=True, vmem_limit_bytes=56 * 1024 * 1024
        ),
    )(features, weight, cotangent, cols, counts, tiles)
    return pl.pallas_call(
        finish,
        out_shape=tuple(jax.ShapeDtypeStruct(r.shape, r.dtype) for r in results),
        in_specs=[spec] * 3,
        out_specs=(spec,) * 3,
        compiler_params=pltpu.CompilerParams(vmem_limit_bytes=63 * 1024 * 1024),
    )(*results)


def solution(mesh):
    return jax.shard_map(
        body,
        mesh=mesh,
        in_specs=(
            P(("section", "rep"), None),
            P(),
            P(("section", "rep"), None),
            P("section", "rep", None, None, None, None),
            P("section", "rep", None, None),
            P("section", "rep", None),
        ),
        out_specs=(P(("section", "rep"), None), P(("section", "rep"), None), P()),
        check_vma=False,
    )
```

```python
import jax
import jax.numpy as jnp
from jax import lax
from jax.experimental import pallas as pl
from jax.experimental.pallas import tpu as pltpu
from jax.sharding import PartitionSpec as P

MESH = pl.DeviceIdType.MESH
F32 = jnp.float32
BF16 = jnp.bfloat16
NX, NY, NZ = 4, 8, 8
ZH = NZ // 2
GROUP = 2 * NX
SLOTS = 2
TILE = 128
D = 256
TERMS = ZH * GROUP * SLOTS
ZERO = TERMS


def device(x, y, z, k):
    return ((x // 2) * (2 * NZ) + z * 2 + k, y * 2 + x % 2)


def kernel(
    feat_ref, weight_ref, cot_ref, cols_ref, counts_ref, tiles_ref,
    out_ref, gf_ref, gw_ref,
    tiles_rx, meta_tx, meta_rx, meta_sm, prev_sm, last_sm,
    feats, part_tx, part_rx, grad_tx, grad_rx, chain,
    sib_tx, sib_rx, plus_tx, plus_rx, minus_tx, minus_rx, zred_tx, zred_rx,
    gw1_tx, gw1_rx, gw2_tx, gw2_rx, gw3_rx, gw4_rx, gw5_rx,
    local_sem, tile_s, tile_r, meta_s, meta_r, agz_s, agz_r,
    agp_s, agp_r, agm_s, agm_r, agd_s, agd_r, part_s, part_r, grad_s, grad_r,
    sib_s, sib_r, plus_s, plus_r, minus_s, minus_r, zred_s, zred_r,
    gw_s, gw_r,
):
    section, rep = lax.axis_index("section"), lax.axis_index("rep")
    xh, z, k = section // (2 * NZ), (section // 2) % NZ, section % 2
    y, xl = rep // 2, rep % 2
    x = 2 * xh + xl
    zp, zh = z % 2, z // 2
    member = x * 2 + k
    turn = 1 - 2 * k
    zpair = (z + turn * (1 - 2 * zp) + NZ) % NZ
    mine = x * 2 + zp
    sibling = device(x, y, z, 1 - k)

    def partner(j):
        return device(2 * xh + k, y, j * 2 + zp, xl)

    def yp(j):
        return (y + turn * j + 2 * NY) % NY

    def group(o):
        h = o // 2
        px, pz = (x + h + (h // 2) * (1 - 2 * (h % 2))) % NX, (zp + o % 2) % 2
        return px, pz, px * 2 + pz

    def peer(o):
        px, pz, p = group(o)
        return px, pz, p, device(px, y, zpair if o % 2 else z, k)

    def copy(src, dst, send, recv, dev):
        return pltpu.make_async_remote_copy(
            src_ref=src, dst_ref=dst, send_sem=send, recv_sem=recv,
            device_id=dev, device_id_type=MESH,
        )

    sent = []

    def send(src, dst, ssem, rsem, dev):
        c = copy(src, dst, ssem, rsem, dev)
        c.start()
        sent.append(c)

    def arrived(dst, ssem, rsem):
        copy(dst, dst, ssem, rsem, sibling).wait_recv()

    ypeers = [(y + i) % NY for i in range(1, NY)]
    zpeers = [(z + i) % NZ for i in range(1, NZ)]
    mpeers = [(member + i) % GROUP for i in range(1, GROUP)]

    own_tiles = pltpu.make_async_copy(
        tiles_ref.at[x // 2, :, zp, x % 2], tiles_rx.at[mine], local_sem.at[0]
    )
    own_tiles.start()

    barrier = pltpu.get_barrier_semaphore()
    everyone = (
        [device(x, j, z, k) for j in ypeers]
        + [device(x, y, j, k) for j in zpeers]
        + [device(j // 2, y, z, j % 2) for j in mpeers]
        + [peer(o)[3] for o in (3, 5, 7)]
        + [partner((zh + i) % ZH) for i in range(1, ZH)]
    )
    for dev in everyone:
        pl.semaphore_signal(barrier, inc=1, device_id=dev, device_id_type=MESH)
    pl.semaphore_wait(barrier, len(everyone))

    @pl.when(xl == k)
    def _():
        feats[k, y, zh] = feat_ref[...]

    @pl.when(xl != k)
    def _():
        copy(feat_ref, feats.at[xl, y, zh], agz_s.at[0], agz_r.at[zh], partner(zh)).start()

    zothers = [(zh + i) % ZH for i in range(ZH)]
    for i in range(1, ZH):
        send(feat_ref, feats.at[xl, y, zh], agz_s.at[i], agz_r.at[zh], partner(zothers[i]))

    dead = lax.broadcasted_iota(jnp.int32, (SLOTS, 32), 0) >= counts_ref[...]
    meta_tx[...] = jnp.zeros_like(meta_tx)
    meta_tx[0:SLOTS, 0:32] = cols_ref[...] + jnp.where(dead, 2 * NY, 0)
    for o in range(1, GROUP):
        px, pz, p, dev = peer(o)
        send(meta_tx, meta_rx.at[mine], meta_s.at[o], meta_r.at[mine], dev)
    meta_rx[mine] = meta_tx[...]

    def send_tiles(c):
        for o in range(1, GROUP):
            px, pz, p, dev = peer(o)
            send(
                tiles_ref.at[px // 2, c, pz, px % 2], tiles_rx.at[mine, c],
                tile_s.at[o, c], tile_r.at[mine, c], dev,
            )

    up, down = device(x, yp(1), z, k), device(x, yp(-1), z, k)

    def gather_plus(s, i):
        c, j = yp(-s), zothers[i]
        send(feats.at[k, c, j], feats.at[k, c, j], agp_s.at[s, i], agp_r.at[s, i], up)

    def gather_minus(s, i):
        c, j = yp(s), zothers[i]
        send(feats.at[k, c, j], feats.at[k, c, j], agm_s.at[s, i], agm_r.at[s, i], down)

    def gather_sibling(j):
        c = yp(j)
        send(feats.at[k, c], feats.at[k, c], agd_s.at[j % NY], agd_r.at[c], sibling)

    send_tiles(0)
    for i in range(ZH):
        j = zothers[i]
        if i == 0:
            @pl.when(xl != k)
            def _():
                arrived(feats.at[k, y, zh], agz_s.at[0], agz_r.at[zh])
        else:
            arrived(feats.at[k, y, j], agz_s.at[i], agz_r.at[j])
        gather_plus(0, i)
        gather_minus(0, i)
    gather_sibling(0)
    send_tiles(1)
    for s in range(4):
        for i in range(ZH):
            arrived(feats.at[k, yp(-s - 1), zothers[i]], agp_s.at[s, i], agp_r.at[s, i])
            if s < 3:
                gather_plus(s + 1, i)
                arrived(feats.at[k, yp(s + 1), zothers[i]], agm_s.at[s, i], agm_r.at[s, i])
                if s < 2:
                    gather_minus(s + 1, i)
        gather_sibling(-s - 1)
        if s < 3:
            gather_sibling(s + 1)
        if s < 2:
            send_tiles(s + 2)

    for o in range(1, GROUP):
        p = peer(o)[2]
        arrived(meta_rx.at[p], meta_s.at[o], meta_r.at[p])
    to_scalar = pltpu.make_async_copy(meta_rx, meta_sm, local_sem.at[1])
    to_scalar.start()
    to_scalar.wait()

    def column_section(c):
        return (x // 2) * (2 * NZ) + c * 4 + zp * 2 + x % 2

    @pl.loop(0, ZH * 2 * NY)
    def _(q):
        last_sm[q] = ZERO

    @pl.loop(0, TERMS)
    def _(i):
        c, o, s = i // (GROUP * SLOTS), (i // SLOTS) % GROUP, i % SLOTS
        col = meta_sm[group(o)[2], s, column_section(c)] % (2 * NY)
        prev_sm[i] = last_sm[c * 2 * NY + col]
        for q in range(2 * NY):
            last_sm[c * 2 * NY + q] = jnp.where(col == q, i, last_sm[c * 2 * NY + q])

    chain[ZERO] = jnp.zeros((D, TILE), F32)

    for j in range(NY):
        c = (y + j) % NY
        arrived(feats.at[1 - k, c], agd_s.at[0], agd_r.at[c])

    def live_tiles(p, c):
        tiles, codes = [], []
        for s in range(SLOTS):
            code = meta_sm[p, s, column_section(c)]
            tile = tiles_rx[p, c, s]
            tiles.append(jnp.where(code < 2 * NY, tile, jnp.zeros_like(tile)))
            codes.append(code % (2 * NY))
        return jnp.concatenate(tiles, axis=1), codes

    total = None
    for o in (1, 2, 3, 4, 5, 6, 7, 0):
        px, pz, p, dev = peer(o)
        if o == 0:
            own_tiles.wait()
        else:
            for c in range(ZH):
                arrived(tiles_rx.at[p, c], tile_s.at[o, c], tile_r.at[p, c])
        acc = jnp.zeros((TILE, D), F32)
        for c in range(ZH):
            pair, cols = live_tiles(p, c)
            rows = jnp.concatenate([feats[col % 2, col // 2, c] for col in cols], axis=0)
            acc += jnp.dot(pair, rows, preferred_element_type=F32)
        if o == 0:
            total = acc
        else:
            part_tx[o] = acc.astype(BF16)
            send(part_tx.at[o], part_rx.at[mine], part_s.at[o], part_r.at[mine], dev)
    for o in range(1, GROUP):
        p = peer(o)[2]
        arrived(part_rx.at[p], part_s.at[o], part_r.at[p])
        total += part_rx[p].astype(F32)

    aggregated = total.astype(BF16)
    weight = weight_ref[...]
    pre = jnp.dot(aggregated, weight, preferred_element_type=F32)
    sig = lax.logistic(pre)
    out_ref[...] = (pre * sig).astype(BF16)
    grad_pre = (cot_ref[...].astype(F32) * sig * (1.0 + pre * (1.0 - sig))).astype(BF16)
    grad_tx[...] = lax.dot_general(
        weight, grad_pre, (((1,), (1,)), ((), ())), preferred_element_type=F32
    ).astype(BF16)
    for o in range(1, GROUP):
        px, pz, p, dev = peer(o)
        send(grad_tx, grad_rx.at[mine], grad_s.at[o], grad_r.at[mine], dev)

    terms = lax.dot_general(
        aggregated, grad_pre, (((0,), (0,)), ((), ())), preferred_element_type=F32
    )
    for i in range(NZ):
        for j in range(GROUP):
            r0, c0 = i * 32 + (j % 4) * 8, (j // 4) * 128
            gw1_tx[i, j] = terms[r0:r0 + 8, c0:c0 + 128]
    for i, j in enumerate(zpeers):
        send(gw1_tx.at[j], gw1_rx.at[z], gw_s.at[0, i], gw_r.at[0, z], device(x, y, j, k))
    gw1_rx[z] = gw1_tx[z]

    for o in range(GROUP):
        px, pz, p, dev = peer(o)
        if o == 0:
            grads = grad_tx[...]
        else:
            arrived(grad_rx.at[p], grad_s.at[o], grad_r.at[p])
            grads = grad_rx[p]
        for c in range(ZH):
            pair, cols = live_tiles(p, c)
            both = jnp.dot(grads, pair, preferred_element_type=F32)
            for s in range(SLOTS):
                i = c * GROUP * SLOTS + o * SLOTS + s
                chain[i] = both[:, s * TILE:(s + 1) * TILE] + chain[prev_sm[i]]

    def block(c, yy, half):
        return chain[last_sm[c * 2 * NY + yy * 2 + half]]

    def send_half(j):
        yy = yp(j)
        for c in range(ZH):
            sib_tx[yy, c] = block(c, yy, 1 - k).astype(BF16)
        send(sib_tx.at[yy], sib_rx.at[yy], sib_s.at[j % NY], sib_r.at[yy], sibling)

    def both_cores(yy, c):
        return block(c, yy, k) + sib_rx[yy, c].astype(F32)

    def reduce_step(s, target, tx, rx, ssem, rsem, dev):
        arrived(sib_rx.at[target], sib_s.at[0], sib_r.at[target])
        for c in range(ZH):
            value = both_cores(target, c)
            if s > 0:
                arrived(rx.at[s - 1, c], ssem.at[s - 1, c], rsem.at[s - 1, c])
                value += rx[s - 1, c].astype(F32)
            tx[s, c] = value.astype(BF16)
            send(tx.at[s, c], rx.at[s, c], ssem.at[s, c], rsem.at[s, c], dev)

    def weight_round(s):
        if s == 0:
            for i, j in enumerate(zpeers):
                arrived(gw1_rx.at[j], gw_s.at[0, i], gw_r.at[0, j])
            gw2_tx[...] = jnp.sum(gw1_rx[...], axis=0)
            for i, j in enumerate(mpeers):
                send(gw2_tx.at[j], gw2_rx.at[member], gw_s.at[1, i], gw_r.at[1, member], device(j // 2, y, z, j % 2))
            gw2_rx[member] = gw2_tx[member]
        elif s == 1:
            for i, j in enumerate(mpeers):
                arrived(gw2_rx.at[j], gw_s.at[1, i], gw_r.at[1, j])
            gw3_rx[y] = jnp.sum(gw2_rx[...], axis=0)
            for i, j in enumerate(ypeers):
                send(gw3_rx.at[y], gw3_rx.at[y], gw_s.at[2, i], gw_r.at[2, y], device(x, j, z, k))
        elif s == 2:
            for i, j in enumerate(ypeers):
                arrived(gw3_rx.at[j], gw_s.at[2, i], gw_r.at[2, j])
            gw4_rx[member] = jnp.sum(gw3_rx[...], axis=0)
            for i, j in enumerate(mpeers):
                send(gw4_rx.at[member], gw4_rx.at[member], gw_s.at[3, i], gw_r.at[3, member], device(j // 2, y, z, j % 2))
        else:
            for i, j in enumerate(mpeers):
                arrived(gw4_rx.at[j], gw_s.at[3, i], gw_r.at[3, j])
            gw5_rx[z] = gw4_rx[...]
            for i, j in enumerate(zpeers):
                send(gw5_rx.at[z], gw5_rx.at[z], gw_s.at[4, i], gw_r.at[4, z], device(x, y, j, k))

    for s, halves in enumerate(((4, 3), (-3, 2), (-2, 1), (-1, 0))):
        for j in halves:
            send_half(j)
        reduce_step(s, yp(4 - s), plus_tx, plus_rx, plus_s, plus_r, up)
        if s < 3:
            reduce_step(s, yp(s - 3), minus_tx, minus_rx, minus_s, minus_r, down)
        weight_round(s)

    arrived(sib_rx.at[y], sib_s.at[0], sib_r.at[y])
    for c in range(ZH):
        arrived(plus_rx.at[3, c], plus_s.at[3, c], plus_r.at[3, c])
        arrived(minus_rx.at[2, c], minus_s.at[2, c], minus_r.at[2, c])
    for i in (1, 2, 3, 0):
        j = zothers[i]
        value = both_cores(y, j) + plus_rx[3, j].astype(F32) + minus_rx[2, j].astype(F32)
        zred_tx[i] = value.astype(BF16)
        if i > 0:
            send(zred_tx.at[i], zred_rx.at[zh], zred_s.at[i], zred_r.at[zh], partner(j))

    @pl.when(xl == k)
    def _():
        zred_rx[zh] = zred_tx[0]

    @pl.when(xl != k)
    def _():
        copy(zred_tx.at[0], zred_rx.at[zh], zred_s.at[0], zred_r.at[zh], partner(zh)).start()

    for i, j in enumerate(zpeers):
        arrived(gw5_rx.at[j], gw_s.at[4, i], gw_r.at[4, j])
    scale = 1.0 / 256.0
    for i in range(NZ):
        for j in range(GROUP):
            r0, c0 = i * 32 + (j % 4) * 8, (j // 4) * 128
            gw_ref[r0:r0 + 8, c0:c0 + 128] = gw5_rx[i, j] * scale

    for i in range(1, ZH):
        arrived(zred_rx.at[zothers[i]], zred_s.at[i], zred_r.at[zothers[i]])

    @pl.when(xl != k)
    def _():
        arrived(zred_rx.at[zh], zred_s.at[0], zred_r.at[zh])

    gf_ref[...] = jnp.sum(zred_rx[...].astype(F32), axis=0).T.astype(BF16)

    @pl.when(xl != k)
    def _():
        copy(zred_tx.at[0], zred_rx.at[zh], zred_s.at[0], zred_r.at[zh], partner(zh)).wait_send()
        copy(feat_ref, feats.at[xl, y, zh], agz_s.at[0], agz_r.at[zh], partner(zh)).wait_send()

    for c in sent:
        c.wait_send()


def finish(out_in, gf_in, gw_in, out_ref, gf_ref, gw_ref):
    out_ref[...] = out_in[...]
    gf_ref[...] = gf_in[...]
    gw_ref[...] = gw_in[...]


def body(features, weight, cotangent, tile_values, tile_cols, tile_counts):
    cols = tile_cols.reshape(32, SLOTS).T
    counts = tile_counts.reshape(1, 32)
    tiles = tile_values.reshape(2, ZH, 2, 2, SLOTS, TILE, TILE)
    dma, vmem = pltpu.SemaphoreType.DMA, pltpu.VMEM
    spec = pl.BlockSpec(memory_space=pltpu.VMEM)
    block = (D, TILE)
    results = pl.pallas_call(
        kernel,
        out_shape=(
            jax.ShapeDtypeStruct((TILE, D), BF16),
            jax.ShapeDtypeStruct((TILE, D), BF16),
            jax.ShapeDtypeStruct((D, D), F32),
        ),
        in_specs=[spec] * 5 + [pl.BlockSpec(memory_space=pl.ANY)],
        out_specs=(spec,) * 3,
        scratch_shapes=[
            vmem((GROUP, ZH, SLOTS, TILE, TILE), BF16),
            vmem((8, 128), jnp.int32),
            vmem((GROUP, 8, 128), jnp.int32),
            pltpu.SMEM((GROUP, 8, 128), jnp.int32),
            pltpu.SMEM((TERMS,), jnp.int32),
            pltpu.SMEM((ZH * 2 * NY,), jnp.int32),
            vmem((2, NY, ZH, TILE, D), BF16),
            vmem((GROUP, TILE, D), BF16),
            vmem((GROUP, TILE, D), BF16),
            vmem(block, BF16),
            vmem((GROUP,) + block, BF16),
            vmem((TERMS + 1,) + block, F32),
            vmem((NY, ZH) + block, BF16),
            vmem((NY, ZH) + block, BF16),
            vmem((4, ZH) + block, BF16),
            vmem((4, ZH) + block, BF16),
            vmem((3, ZH) + block, BF16),
            vmem((3, ZH) + block, BF16),
            vmem((ZH,) + block, BF16),
            vmem((ZH,) + block, BF16),
            vmem((NZ, GROUP, 8, 128), F32),
            vmem((NZ, GROUP, 8, 128), F32),
            vmem((GROUP, 8, 128), F32),
            vmem((GROUP, 8, 128), F32),
            vmem((NY, 8, 128), F32),
            vmem((GROUP, 8, 128), F32),
            vmem((NZ, GROUP, 8, 128), F32),
            dma((2,)),
            dma((GROUP, ZH)), dma((GROUP, ZH)),
            dma((GROUP,)), dma((GROUP,)),
            dma((ZH,)), dma((ZH,)),
            dma((4, ZH)), dma((4, ZH)),
            dma((3, ZH)), dma((3, ZH)),
            dma((NY,)), dma((NY,)),
            dma((GROUP,)), dma((GROUP,)),
            dma((GROUP,)), dma((GROUP,)),
            dma((NY,)), dma((NY,)),
            dma((4, ZH)), dma((4, ZH)),
            dma((3, ZH)), dma((3, ZH)),
            dma((ZH,)), dma((ZH,)),
            dma((5, 8)), dma((5, 8)),
        ],
        compiler_params=pltpu.CompilerParams(
            collective_id=0, has_side_effects=True, vmem_limit_bytes=56 * 1024 * 1024
        ),
    )(features, weight, cotangent, cols, counts, tiles)
    return pl.pallas_call(
        finish,
        out_shape=tuple(jax.ShapeDtypeStruct(r.shape, r.dtype) for r in results),
        in_specs=[spec] * 3,
        out_specs=(spec,) * 3,
        compiler_params=pltpu.CompilerParams(vmem_limit_bytes=63 * 1024 * 1024),
    )(*results)


def solution(mesh):
    return jax.shard_map(
        body,
        mesh=mesh,
        in_specs=(
            P(("section", "rep"), None),
            P(),
            P(("section", "rep"), None),
            P("section", "rep", None, None, None, None),
            P("section", "rep", None, None),
            P("section", "rep", None),
        ),
        out_specs=(P(("section", "rep"), None), P(("section", "rep"), None), P()),
        check_vma=False,
    )
```

```python
import jax
import jax.numpy as jnp
from jax import lax
from jax.experimental import pallas as pl
from jax.experimental.pallas import tpu as pltpu
from jax.sharding import PartitionSpec as P

MESH = pl.DeviceIdType.MESH
F32 = jnp.float32
BF16 = jnp.bfloat16
NX, NY, NZ = 4, 8, 8
ZH = NZ // 2
GROUP = 2 * NX
SLOTS = 2
TILE = 128
D = 256
TERMS = ZH * GROUP * SLOTS
ORDER = (0, 4, 2, 1, 6, 5, 3, 7)
ZERO = TERMS


def device(x, y, z, k):
    return ((x // 2) * (2 * NZ) + z * 2 + k, y * 2 + x % 2)


def kernel(
    feat_ref, weight_ref, cot_ref, cols_ref, counts_ref, tiles_ref,
    out_ref, gf_ref, gw_ref,
    tiles_rx, meta_tx, meta_rx, meta_sm, prev_sm, last_sm,
    feats, relay_rx, part_tx, part_pass, part_rx, grad_tx, grad_rx, chain,
    sib_tx, sib_rx, plus_tx, plus_rx, minus_tx, minus_rx, zred_tx, zred_rx,
    gw1_tx, gw1_rx, gw2_tx, gw2_rx, gw3_rx, gw4_rx, gw5_rx,
    local_sem, relay_s, relay_r, pass_r, tile_s, tile_r, meta_s, meta_r, agz_s, agz_r,
    agp_s, agp_r, agm_s, agm_r, agd_s, agd_r, part_s, part_r, grad_s, grad_r,
    sib_s, sib_r, plus_s, plus_r, minus_s, minus_r, zred_s, zred_r,
    gw_s, gw_r,
):
    section, rep = lax.axis_index("section"), lax.axis_index("rep")
    xh, z, k = section // (2 * NZ), (section // 2) % NZ, section % 2
    y, xl = rep // 2, rep % 2
    x = 2 * xh + xl
    zp, zh = z % 2, z // 2
    member = x * 2 + k
    turn = 1 - 2 * k
    zpair = (z + turn * (1 - 2 * zp) + NZ) % NZ
    mine = x * 2 + zp
    sibling = device(x, y, z, 1 - k)

    def partner(j):
        return device(2 * xh + k, y, j * 2 + zp, xl)

    def yp(j):
        return (y + turn * j + 2 * NY) % NY

    def group(o):
        h = o // 2
        px = (x + turn * (h + (h // 2) * (1 - 2 * (h % 2))) + 2 * NX) % NX
        pz = (zp + o % 2) % 2
        return px, pz, px * 2 + pz

    def peer(o):
        px, pz, p = group(o)
        return px, pz, p, device(px, y, zpair if o % 2 else z, k)

    def copy(src, dst, send, recv, dev):
        return pltpu.make_async_remote_copy(
            src_ref=src, dst_ref=dst, send_sem=send, recv_sem=recv,
            device_id=dev, device_id_type=MESH,
        )

    sent = []

    def send(src, dst, ssem, rsem, dev):
        c = copy(src, dst, ssem, rsem, dev)
        c.start()
        sent.append(c)

    def arrived(dst, ssem, rsem):
        copy(dst, dst, ssem, rsem, sibling).wait_recv()

    ypeers = [(y + i) % NY for i in range(1, NY)]
    zpeers = [(z + i) % NZ for i in range(1, NZ)]
    mpeers = [(member + i) % GROUP for i in range(1, GROUP)]

    own_tiles = pltpu.make_async_copy(
        tiles_ref.at[x // 2, :, zp, x % 2], tiles_rx.at[mine], local_sem.at[0]
    )
    own_tiles.start()

    barrier = pltpu.get_barrier_semaphore()
    everyone = (
        [device(x, j, z, k) for j in ypeers]
        + [device(x, y, j, k) for j in zpeers]
        + [device(j // 2, y, z, j % 2) for j in mpeers]
        + [peer(o)[3] for o in (3, 5, 7)]
        + [partner((zh + i) % ZH) for i in range(1, ZH)]
    )
    for dev in everyone:
        pl.semaphore_signal(barrier, inc=1, device_id=dev, device_id_type=MESH)
    pl.semaphore_wait(barrier, len(everyone))

    @pl.when(xl == k)
    def _():
        feats[k, y, zh] = feat_ref[...]

    @pl.when(xl != k)
    def _():
        copy(feat_ref, feats.at[xl, y, zh], agz_s.at[0], agz_r.at[zh], partner(zh)).start()

    zothers = [(zh + i) % ZH for i in range(ZH)]
    for i in range(1, ZH):
        send(feat_ref, feats.at[xl, y, zh], agz_s.at[i], agz_r.at[zh], partner(zothers[i]))

    dead = lax.broadcasted_iota(jnp.int32, (SLOTS, 32), 0) >= counts_ref[...]
    meta_tx[...] = jnp.zeros_like(meta_tx)
    meta_tx[0:SLOTS, 0:32] = cols_ref[...] + jnp.where(dead, 2 * NY, 0)
    for o in range(1, GROUP):
        px, pz, p, dev = peer(o)
        send(meta_tx, meta_rx.at[mine], meta_s.at[o], meta_r.at[mine], dev)
    meta_rx[mine] = meta_tx[...]

    def send_tiles(c):
        for o in (6, 7, 2, 3, 4, 5, 1):
            px, pz, p, dev = peer(o)
            dst, rsem = tiles_rx.at[mine, c], tile_r.at[mine, c]
            if o >= 6:
                dst, rsem, dev = relay_rx.at[o - 6, c], relay_r.at[o - 6, c], peer(2)[3]
            send(tiles_ref.at[px // 2, c, pz, px % 2], dst, tile_s.at[o, c], rsem, dev)

    before = group(4)[2]

    def pass_tiles(c):
        for o in range(2):
            arrived(relay_rx.at[o, c], relay_s.at[o, c], relay_r.at[o, c])
            send(relay_rx.at[o, c], tiles_rx.at[before, c], relay_s.at[o, c], tile_r.at[before, c], peer(2 + o)[3])

    up, down = device(x, yp(1), z, k), device(x, yp(-1), z, k)

    def gather_plus(s, i):
        c, j = yp(-s), zothers[i]
        send(feats.at[k, c, j], feats.at[k, c, j], agp_s.at[s, i], agp_r.at[s, i], up)

    def gather_minus(s, i):
        c, j = yp(s), zothers[i]
        send(feats.at[k, c, j], feats.at[k, c, j], agm_s.at[s, i], agm_r.at[s, i], down)

    def gather_sibling(j):
        c = yp(j)
        send(feats.at[k, c], feats.at[k, c], agd_s.at[j % NY], agd_r.at[c], sibling)

    send_tiles(0)
    for i in range(ZH):
        j = zothers[i]
        if i == 0:
            @pl.when(xl != k)
            def _():
                arrived(feats.at[k, y, zh], agz_s.at[0], agz_r.at[zh])
        else:
            arrived(feats.at[k, y, j], agz_s.at[i], agz_r.at[j])
        gather_plus(0, i)
        gather_minus(0, i)
    gather_sibling(0)
    send_tiles(1)
    for s in range(4):
        for i in range(ZH):
            arrived(feats.at[k, yp(-s - 1), zothers[i]], agp_s.at[s, i], agp_r.at[s, i])
            if s < 3:
                gather_plus(s + 1, i)
                arrived(feats.at[k, yp(s + 1), zothers[i]], agm_s.at[s, i], agm_r.at[s, i])
                if s < 2:
                    gather_minus(s + 1, i)
        gather_sibling(-s - 1)
        if s < 3:
            gather_sibling(s + 1)
        if s < 2:
            send_tiles(s + 2)
        pass_tiles(s)

    for o in range(1, GROUP):
        p = peer(o)[2]
        arrived(meta_rx.at[p], meta_s.at[o], meta_r.at[p])
    to_scalar = pltpu.make_async_copy(meta_rx, meta_sm, local_sem.at[1])
    to_scalar.start()
    to_scalar.wait()

    def column_section(c):
        return (x // 2) * (2 * NZ) + c * 4 + zp * 2 + x % 2

    @pl.loop(0, ZH * 2 * NY)
    def _(q):
        last_sm[q] = ZERO

    for n, o in enumerate(ORDER):
        p = group(o)[2]

        @pl.loop(0, ZH * SLOTS)
        def _(t):
            c, s = t // SLOTS, t % SLOTS
            i = c * (GROUP * SLOTS) + n * SLOTS + s
            col = meta_sm[p, s, column_section(c)] % (2 * NY)
            prev_sm[i] = last_sm[c * 2 * NY + col]
            for q in range(2 * NY):
                last_sm[c * 2 * NY + q] = jnp.where(col == q, i, last_sm[c * 2 * NY + q])

    chain[ZERO] = jnp.zeros((D, TILE), F32)

    for j in range(NY):
        c = (y + j) % NY
        arrived(feats.at[1 - k, c], agd_s.at[0], agd_r.at[c])

    def live_tiles(p, c):
        tiles, codes = [], []
        for s in range(SLOTS):
            code = meta_sm[p, s, column_section(c)]
            tile = tiles_rx[p, c, s]
            tiles.append(jnp.where(code < 2 * NY, tile, jnp.zeros_like(tile)))
            codes.append(code % (2 * NY))
        return jnp.concatenate(tiles, axis=1), codes

    total = None
    for o in (6, 7, 4, 5, 1, 2, 3, 0):
        px, pz, p, dev = peer(o)
        if o == 0:
            own_tiles.wait()
        else:
            for c in range(ZH):
                arrived(tiles_rx.at[p, c], tile_s.at[o, c], tile_r.at[p, c])
        acc = jnp.zeros((TILE, D), F32)
        for c in range(ZH):
            pair, cols = live_tiles(p, c)
            rows = jnp.concatenate([feats[col % 2, col // 2, c] for col in cols], axis=0)
            acc += jnp.dot(pair, rows, preferred_element_type=F32)
        if o == 0:
            total = acc
        else:
            if o in (2, 3):
                arrived(part_pass.at[o - 2], part_s.at[o], pass_r.at[o - 2])
                acc += part_pass[o - 2].astype(F32)
            part_tx[o] = acc.astype(BF16)
            dst, rsem = part_rx.at[mine], part_r.at[mine]
            if o >= 6:
                dst, rsem, dev = part_pass.at[o - 6], pass_r.at[o - 6], peer(2)[3]
            send(part_tx.at[o], dst, part_s.at[o], rsem, dev)
    for o in range(1, 6):
        p = peer(o)[2]
        arrived(part_rx.at[p], part_s.at[o], part_r.at[p])
        total += part_rx[p].astype(F32)

    aggregated = total.astype(BF16)
    weight = weight_ref[...]
    pre = jnp.dot(aggregated, weight, preferred_element_type=F32)
    sig = lax.logistic(pre)
    out_ref[...] = (pre * sig).astype(BF16)
    grad_pre = (cot_ref[...].astype(F32) * sig * (1.0 + pre * (1.0 - sig))).astype(BF16)
    grad_tx[...] = lax.dot_general(
        weight, grad_pre, (((1,), (1,)), ((), ())), preferred_element_type=F32
    ).astype(BF16)
    for n, o in enumerate((4, 2, 1)):
        send(grad_tx, grad_rx.at[mine], grad_s.at[n], grad_r.at[mine], peer(o)[3])

    def pass_grads(o, n, targets):
        p = group(o)[2]
        arrived(grad_rx.at[p], grad_s.at[n], grad_r.at[p])
        for i, t in enumerate(targets):
            send(grad_rx.at[p], grad_rx.at[p], grad_s.at[n + i], grad_r.at[p], peer(t)[3])

    terms = lax.dot_general(
        aggregated, grad_pre, (((0,), (0,)), ((), ())), preferred_element_type=F32
    )
    for i in range(NZ):
        for j in range(GROUP):
            r0, c0 = i * 32 + (j % 4) * 8, (j // 4) * 128
            gw1_tx[i, j] = terms[r0:r0 + 8, c0:c0 + 128]
    for i, j in enumerate(zpeers):
        send(gw1_tx.at[j], gw1_rx.at[z], gw_s.at[0, i], gw_r.at[0, z], device(x, y, j, k))
    gw1_rx[z] = gw1_tx[z]

    for n, o in enumerate(ORDER):
        p = group(o)[2]
        if n == 1:
            pass_grads(4, 3, (2, 1))
            pass_grads(2, 5, (1,))
        elif n == 4:
            pass_grads(6, 6, (1,))
        elif o in (1, 5, 3, 7):
            arrived(grad_rx.at[p], grad_s.at[0], grad_r.at[p])
        grads = grad_rx[p] if o else grad_tx[...]
        for c in range(ZH):
            pair, cols = live_tiles(p, c)
            both = jnp.dot(grads, pair, preferred_element_type=F32)
            for s in range(SLOTS):
                i = c * GROUP * SLOTS + n * SLOTS + s
                chain[i] = both[:, s * TILE:(s + 1) * TILE] + chain[prev_sm[i]]

    def block(c, yy, half):
        return chain[last_sm[c * 2 * NY + yy * 2 + half]]

    def send_half(j):
        yy = yp(j)
        for c in range(ZH):
            sib_tx[yy, c] = block(c, yy, 1 - k).astype(BF16)
        send(sib_tx.at[yy], sib_rx.at[yy], sib_s.at[j % NY], sib_r.at[yy], sibling)

    def both_cores(yy, c):
        return block(c, yy, k) + sib_rx[yy, c].astype(F32)

    def reduce_step(s, target, tx, rx, ssem, rsem, dev):
        arrived(sib_rx.at[target], sib_s.at[0], sib_r.at[target])
        for c in range(ZH):
            value = both_cores(target, c)
            if s > 0:
                arrived(rx.at[s - 1, c], ssem.at[s - 1, c], rsem.at[s - 1, c])
                value += rx[s - 1, c].astype(F32)
            tx[s, c] = value.astype(BF16)
            send(tx.at[s, c], rx.at[s, c], ssem.at[s, c], rsem.at[s, c], dev)

    def weight_round(s):
        if s == 0:
            for i, j in enumerate(zpeers):
                arrived(gw1_rx.at[j], gw_s.at[0, i], gw_r.at[0, j])
            gw2_tx[...] = jnp.sum(gw1_rx[...], axis=0)
            for i, j in enumerate(mpeers):
                send(gw2_tx.at[j], gw2_rx.at[member], gw_s.at[1, i], gw_r.at[1, member], device(j // 2, y, z, j % 2))
            gw2_rx[member] = gw2_tx[member]
        elif s == 1:
            for i, j in enumerate(mpeers):
                arrived(gw2_rx.at[j], gw_s.at[1, i], gw_r.at[1, j])
            gw3_rx[y] = jnp.sum(gw2_rx[...], axis=0)
            for i, j in enumerate(ypeers):
                send(gw3_rx.at[y], gw3_rx.at[y], gw_s.at[2, i], gw_r.at[2, y], device(x, j, z, k))
        elif s == 2:
            for i, j in enumerate(ypeers):
                arrived(gw3_rx.at[j], gw_s.at[2, i], gw_r.at[2, j])
            gw4_rx[member] = jnp.sum(gw3_rx[...], axis=0)
            for i, j in enumerate(mpeers):
                send(gw4_rx.at[member], gw4_rx.at[member], gw_s.at[3, i], gw_r.at[3, member], device(j // 2, y, z, j % 2))
        else:
            for i, j in enumerate(mpeers):
                arrived(gw4_rx.at[j], gw_s.at[3, i], gw_r.at[3, j])
            gw5_rx[z] = gw4_rx[...]
            for i, j in enumerate(zpeers):
                send(gw5_rx.at[z], gw5_rx.at[z], gw_s.at[4, i], gw_r.at[4, z], device(x, y, j, k))

    for s, halves in enumerate(((4, 3), (-3, 2), (-2, 1), (-1, 0))):
        for j in halves:
            send_half(j)
        reduce_step(s, yp(4 - s), plus_tx, plus_rx, plus_s, plus_r, up)
        if s < 3:
            reduce_step(s, yp(s - 3), minus_tx, minus_rx, minus_s, minus_r, down)
        weight_round(s)

    arrived(sib_rx.at[y], sib_s.at[0], sib_r.at[y])
    for c in range(ZH):
        arrived(plus_rx.at[3, c], plus_s.at[3, c], plus_r.at[3, c])
        arrived(minus_rx.at[2, c], minus_s.at[2, c], minus_r.at[2, c])
    for i in (1, 2, 3, 0):
        j = zothers[i]
        value = both_cores(y, j) + plus_rx[3, j].astype(F32) + minus_rx[2, j].astype(F32)
        zred_tx[i] = value.astype(BF16)
        if i > 0:
            send(zred_tx.at[i], zred_rx.at[zh], zred_s.at[i], zred_r.at[zh], partner(j))

    @pl.when(xl == k)
    def _():
        zred_rx[zh] = zred_tx[0]

    @pl.when(xl != k)
    def _():
        copy(zred_tx.at[0], zred_rx.at[zh], zred_s.at[0], zred_r.at[zh], partner(zh)).start()

    for i, j in enumerate(zpeers):
        arrived(gw5_rx.at[j], gw_s.at[4, i], gw_r.at[4, j])
    scale = 1.0 / 256.0
    for i in range(NZ):
        for j in range(GROUP):
            r0, c0 = i * 32 + (j % 4) * 8, (j // 4) * 128
            gw_ref[r0:r0 + 8, c0:c0 + 128] = gw5_rx[i, j] * scale

    for i in range(1, ZH):
        arrived(zred_rx.at[zothers[i]], zred_s.at[i], zred_r.at[zothers[i]])

    @pl.when(xl != k)
    def _():
        arrived(zred_rx.at[zh], zred_s.at[0], zred_r.at[zh])

    gf_ref[...] = jnp.sum(zred_rx[...].astype(F32), axis=0).T.astype(BF16)

    @pl.when(xl != k)
    def _():
        copy(zred_tx.at[0], zred_rx.at[zh], zred_s.at[0], zred_r.at[zh], partner(zh)).wait_send()
        copy(feat_ref, feats.at[xl, y, zh], agz_s.at[0], agz_r.at[zh], partner(zh)).wait_send()

    for c in sent:
        c.wait_send()


def finish(out_in, gf_in, gw_in, out_ref, gf_ref, gw_ref):
    out_ref[...] = out_in[...]
    gf_ref[...] = gf_in[...]
    gw_ref[...] = gw_in[...]


def body(features, weight, cotangent, tile_values, tile_cols, tile_counts):
    cols = tile_cols.reshape(32, SLOTS).T
    counts = tile_counts.reshape(1, 32)
    tiles = tile_values.reshape(2, ZH, 2, 2, SLOTS, TILE, TILE)
    dma, vmem = pltpu.SemaphoreType.DMA, pltpu.VMEM
    spec = pl.BlockSpec(memory_space=pltpu.VMEM)
    block = (D, TILE)
    results = pl.pallas_call(
        kernel,
        out_shape=(
            jax.ShapeDtypeStruct((TILE, D), BF16),
            jax.ShapeDtypeStruct((TILE, D), BF16),
            jax.ShapeDtypeStruct((D, D), F32),
        ),
        in_specs=[spec] * 5 + [pl.BlockSpec(memory_space=pl.ANY)],
        out_specs=(spec,) * 3,
        scratch_shapes=[
            vmem((GROUP, ZH, SLOTS, TILE, TILE), BF16),
            vmem((8, 128), jnp.int32),
            vmem((GROUP, 8, 128), jnp.int32),
            pltpu.SMEM((GROUP, 8, 128), jnp.int32),
            pltpu.SMEM((TERMS,), jnp.int32),
            pltpu.SMEM((ZH * 2 * NY,), jnp.int32),
            vmem((2, NY, ZH, TILE, D), BF16),
            vmem((2, ZH, SLOTS, TILE, TILE), BF16),
            vmem((GROUP, TILE, D), BF16),
            vmem((2, TILE, D), BF16),
            vmem((GROUP, TILE, D), BF16),
            vmem(block, BF16),
            vmem((GROUP,) + block, BF16),
            vmem((TERMS + 1,) + block, F32),
            vmem((NY, ZH) + block, BF16),
            vmem((NY, ZH) + block, BF16),
            vmem((4, ZH) + block, BF16),
            vmem((4, ZH) + block, BF16),
            vmem((3, ZH) + block, BF16),
            vmem((3, ZH) + block, BF16),
            vmem((ZH,) + block, BF16),
            vmem((ZH,) + block, BF16),
            vmem((NZ, GROUP, 8, 128), F32),
            vmem((NZ, GROUP, 8, 128), F32),
            vmem((GROUP, 8, 128), F32),
            vmem((GROUP, 8, 128), F32),
            vmem((NY, 8, 128), F32),
            vmem((GROUP, 8, 128), F32),
            vmem((NZ, GROUP, 8, 128), F32),
            dma((2,)),
            dma((2, ZH)), dma((2, ZH)), dma((2,)),
            dma((GROUP, ZH)), dma((GROUP, ZH)),
            dma((GROUP,)), dma((GROUP,)),
            dma((ZH,)), dma((ZH,)),
            dma((4, ZH)), dma((4, ZH)),
            dma((3, ZH)), dma((3, ZH)),
            dma((NY,)), dma((NY,)),
            dma((GROUP,)), dma((GROUP,)),
            dma((GROUP,)), dma((GROUP,)),
            dma((NY,)), dma((NY,)),
            dma((4, ZH)), dma((4, ZH)),
            dma((3, ZH)), dma((3, ZH)),
            dma((ZH,)), dma((ZH,)),
            dma((5, 8)), dma((5, 8)),
        ],
        compiler_params=pltpu.CompilerParams(
            collective_id=0, has_side_effects=True, vmem_limit_bytes=56 * 1024 * 1024
        ),
    )(features, weight, cotangent, cols, counts, tiles)
    return pl.pallas_call(
        finish,
        out_shape=tuple(jax.ShapeDtypeStruct(r.shape, r.dtype) for r in results),
        in_specs=[spec] * 3,
        out_specs=(spec,) * 3,
        compiler_params=pltpu.CompilerParams(vmem_limit_bytes=63 * 1024 * 1024),
    )(*results)


def solution(mesh):
    return jax.shard_map(
        body,
        mesh=mesh,
        in_specs=(
            P(("section", "rep"), None),
            P(),
            P(("section", "rep"), None),
            P("section", "rep", None, None, None, None),
            P("section", "rep", None, None),
            P("section", "rep", None),
        ),
        out_specs=(P(("section", "rep"), None), P(("section", "rep"), None), P()),
        check_vma=False,
    )
```

```python
import jax
import jax.numpy as jnp
from jax import lax
from jax.experimental import pallas as pl
from jax.experimental.pallas import tpu as pltpu
from jax.sharding import PartitionSpec as P

MESH = pl.DeviceIdType.MESH
F32 = jnp.float32
BF16 = jnp.bfloat16
NX, NY, NZ = 4, 8, 8
ZH = NZ // 2
GROUP = 2 * NX
SLOTS = 2
TILE = 128
D = 256
TERMS = ZH * GROUP * SLOTS
ZERO = TERMS


def device(x, y, z, k):
    return ((x // 2) * (2 * NZ) + z * 2 + k, y * 2 + x % 2)


def kernel(
    feat_ref, weight_ref, cot_ref, cols_ref, counts_ref, tiles_ref,
    out_ref, gf_ref, gw_ref,
    tiles_rx, meta_tx, meta_rx, meta_sm, prev_sm, last_sm,
    feats, part_tx, part_rx, grad_tx, grad_rx, chain,
    sib_tx, sib_rx, plus_tx, plus_rx, minus_tx, minus_rx, zred_tx, zred_rx,
    gw1_tx, gw1_rx, gw2_tx, gw2_rx, gw3_rx, gw4_rx, gw5_rx,
    local_sem, tile_s, tile_r, meta_s, meta_r, agz_s, agz_r,
    agp_s, agp_r, agm_s, agm_r, agd_s, agd_r, part_s, part_r, grad_s, grad_r,
    sib_s, sib_r, plus_s, plus_r, minus_s, minus_r, zred_s, zred_r,
    gw_s, gw_r,
):
    section, rep = lax.axis_index("section"), lax.axis_index("rep")
    xh, z, k = section // (2 * NZ), (section // 2) % NZ, section % 2
    y, xl = rep // 2, rep % 2
    x = 2 * xh + xl
    zp, zh = z % 2, z // 2
    member = x * 2 + k
    turn = 1 - 2 * k
    zpair = (z + turn * (1 - 2 * zp) + NZ) % NZ
    mine = x * 2 + zp
    sibling = device(x, y, z, 1 - k)

    def partner(j):
        return device(2 * xh + k, y, j * 2 + zp, xl)

    def yp(j):
        return (y + turn * j + 2 * NY) % NY

    def group(o):
        h = o // 2
        px, pz = (x + h + (h // 2) * (1 - 2 * (h % 2))) % NX, (zp + o % 2) % 2
        return px, pz, px * 2 + pz

    def peer(o):
        px, pz, p = group(o)
        return px, pz, p, device(px, y, zpair if o % 2 else z, k)

    def copy(src, dst, send, recv, dev):
        return pltpu.make_async_remote_copy(
            src_ref=src, dst_ref=dst, send_sem=send, recv_sem=recv,
            device_id=dev, device_id_type=MESH,
        )

    sent = []

    def send(src, dst, ssem, rsem, dev):
        c = copy(src, dst, ssem, rsem, dev)
        c.start()
        sent.append(c)

    def arrived(dst, ssem, rsem):
        copy(dst, dst, ssem, rsem, sibling).wait_recv()

    ypeers = [(y + i) % NY for i in range(1, NY)]
    zpeers = [(z + i) % NZ for i in range(1, NZ)]
    mpeers = [(member + i) % GROUP for i in range(1, GROUP)]

    own_tiles = pltpu.make_async_copy(
        tiles_ref.at[x // 2, :, zp, x % 2], tiles_rx.at[mine], local_sem.at[0]
    )
    own_tiles.start()

    barrier = pltpu.get_barrier_semaphore()
    everyone = (
        [device(x, j, z, k) for j in ypeers]
        + [device(x, y, j, k) for j in zpeers]
        + [device(j // 2, y, z, j % 2) for j in mpeers]
        + [peer(o)[3] for o in (3, 5, 7)]
        + [partner((zh + i) % ZH) for i in range(1, ZH)]
    )
    for dev in everyone:
        pl.semaphore_signal(barrier, inc=1, device_id=dev, device_id_type=MESH)
    pl.semaphore_wait(barrier, len(everyone))

    @pl.when(xl == k)
    def _():
        feats[k, y, zh] = feat_ref[...]

    @pl.when(xl != k)
    def _():
        copy(feat_ref, feats.at[xl, y, zh], agz_s.at[0], agz_r.at[zh], partner(zh)).start()

    zothers = [(zh + i) % ZH for i in range(ZH)]
    for i in range(1, ZH):
        send(feat_ref, feats.at[xl, y, zh], agz_s.at[i], agz_r.at[zh], partner(zothers[i]))

    dead = lax.broadcasted_iota(jnp.int32, (SLOTS, 32), 0) >= counts_ref[...]
    meta_tx[...] = jnp.zeros_like(meta_tx)
    meta_tx[0:SLOTS, 0:32] = cols_ref[...] + jnp.where(dead, 2 * NY, 0)
    for o in range(1, GROUP):
        px, pz, p, dev = peer(o)
        send(meta_tx, meta_rx.at[mine], meta_s.at[o], meta_r.at[mine], dev)
    meta_rx[mine] = meta_tx[...]

    def send_tiles(c):
        for o in range(1, GROUP):
            px, pz, p, dev = peer(o)
            send(
                tiles_ref.at[px // 2, c, pz, px % 2], tiles_rx.at[mine, c],
                tile_s.at[o, c], tile_r.at[mine, c], dev,
            )

    def column_section(c):
        return (x // 2) * (2 * NZ) + c * 4 + zp * 2 + x % 2

    def column_table():
        for o in range(1, GROUP):
            p = peer(o)[2]
            arrived(meta_rx.at[p], meta_s.at[o], meta_r.at[p])
        to_scalar = pltpu.make_async_copy(meta_rx, meta_sm, local_sem.at[1])
        to_scalar.start()
        to_scalar.wait()

        @pl.loop(0, ZH * 2 * NY)
        def _(q):
            last_sm[q] = ZERO

        @pl.loop(0, TERMS)
        def _(i):
            c, o, s = i // (GROUP * SLOTS), (i // SLOTS) % GROUP, i % SLOTS
            col = meta_sm[group(o)[2], s, column_section(c)] % (2 * NY)
            prev_sm[i] = last_sm[c * 2 * NY + col]
            for q in range(2 * NY):
                last_sm[c * 2 * NY + q] = jnp.where(col == q, i, last_sm[c * 2 * NY + q])

        chain[ZERO] = jnp.zeros((D, TILE), F32)

    up, down = device(x, yp(1), z, k), device(x, yp(-1), z, k)

    def gather_plus(s, i):
        c, j = yp(-s), zothers[i]
        send(feats.at[k, c, j], feats.at[k, c, j], agp_s.at[s, i], agp_r.at[s, i], up)

    def gather_minus(s, i):
        c, j = yp(s), zothers[i]
        send(feats.at[k, c, j], feats.at[k, c, j], agm_s.at[s, i], agm_r.at[s, i], down)

    def gather_sibling(j):
        c = yp(j)
        send(feats.at[k, c], feats.at[k, c], agd_s.at[j % NY], agd_r.at[c], sibling)

    send_tiles(0)
    for i in range(ZH):
        j = zothers[i]
        if i == 0:
            @pl.when(xl != k)
            def _():
                arrived(feats.at[k, y, zh], agz_s.at[0], agz_r.at[zh])
        else:
            arrived(feats.at[k, y, j], agz_s.at[i], agz_r.at[j])
        gather_plus(0, i)
        gather_minus(0, i)
    gather_sibling(0)
    send_tiles(1)
    for s in range(4):
        if s == 3:
            column_table()
        for i in range(ZH):
            arrived(feats.at[k, yp(-s - 1), zothers[i]], agp_s.at[s, i], agp_r.at[s, i])
            if s < 3:
                gather_plus(s + 1, i)
                arrived(feats.at[k, yp(s + 1), zothers[i]], agm_s.at[s, i], agm_r.at[s, i])
                if s < 2:
                    gather_minus(s + 1, i)
        gather_sibling(-s - 1)
        if s < 3:
            gather_sibling(s + 1)
        if s < 2:
            send_tiles(s + 2)

    for j in range(NY):
        c = (y + j) % NY
        arrived(feats.at[1 - k, c], agd_s.at[0], agd_r.at[c])

    def live_tiles(p, c):
        tiles, codes = [], []
        for s in range(SLOTS):
            code = meta_sm[p, s, column_section(c)]
            tile = tiles_rx[p, c, s]
            tiles.append(jnp.where(code < 2 * NY, tile, jnp.zeros_like(tile)))
            codes.append(code % (2 * NY))
        return jnp.concatenate(tiles, axis=1), codes

    total = None
    for o in (1, 2, 3, 4, 5, 6, 7, 0):
        px, pz, p, dev = peer(o)
        if o == 0:
            own_tiles.wait()
        else:
            for c in range(ZH):
                arrived(tiles_rx.at[p, c], tile_s.at[o, c], tile_r.at[p, c])
        acc = jnp.zeros((TILE, D), F32)
        for c in range(ZH):
            pair, cols = live_tiles(p, c)
            rows = jnp.concatenate([feats[col % 2, col // 2, c] for col in cols], axis=0)
            acc += jnp.dot(pair, rows, preferred_element_type=F32)
        if o == 0:
            total = acc
        else:
            part_tx[o] = acc.astype(BF16)
            send(part_tx.at[o], part_rx.at[mine], part_s.at[o], part_r.at[mine], dev)
    for o in range(1, GROUP):
        p = peer(o)[2]
        arrived(part_rx.at[p], part_s.at[o], part_r.at[p])
        total += part_rx[p].astype(F32)

    aggregated = total.astype(BF16)
    weight = weight_ref[...]
    pre = jnp.dot(aggregated, weight, preferred_element_type=F32)
    sig = lax.logistic(pre)
    out_ref[...] = (pre * sig).astype(BF16)
    grad_pre = (cot_ref[...].astype(F32) * sig * (1.0 + pre * (1.0 - sig))).astype(BF16)
    grad_tx[...] = lax.dot_general(
        weight, grad_pre, (((1,), (1,)), ((), ())), preferred_element_type=F32
    ).astype(BF16)
    for o in range(1, GROUP):
        px, pz, p, dev = peer(o)
        send(grad_tx, grad_rx.at[mine], grad_s.at[o], grad_r.at[mine], dev)

    terms = lax.dot_general(
        aggregated, grad_pre, (((0,), (0,)), ((), ())), preferred_element_type=F32
    )
    for i in range(NZ):
        for j in range(GROUP):
            r0, c0 = i * 32 + (j % 4) * 8, (j // 4) * 128
            gw1_tx[i, j] = terms[r0:r0 + 8, c0:c0 + 128]
    for i, j in enumerate(zpeers):
        send(gw1_tx.at[j], gw1_rx.at[z], gw_s.at[0, i], gw_r.at[0, z], device(x, y, j, k))
    gw1_rx[z] = gw1_tx[z]

    def weight_round(s):
        if s == 0:
            for i, j in enumerate(zpeers):
                arrived(gw1_rx.at[j], gw_s.at[0, i], gw_r.at[0, j])
            gw2_tx[...] = jnp.sum(gw1_rx[...], axis=0)
            for i, j in enumerate(mpeers):
                send(gw2_tx.at[j], gw2_rx.at[member], gw_s.at[1, i], gw_r.at[1, member], device(j // 2, y, z, j % 2))
            gw2_rx[member] = gw2_tx[member]
        elif s == 1:
            for i, j in enumerate(mpeers):
                arrived(gw2_rx.at[j], gw_s.at[1, i], gw_r.at[1, j])
            gw3_rx[y] = jnp.sum(gw2_rx[...], axis=0)
            for i, j in enumerate(ypeers):
                send(gw3_rx.at[y], gw3_rx.at[y], gw_s.at[2, i], gw_r.at[2, y], device(x, j, z, k))
        elif s == 2:
            for i, j in enumerate(ypeers):
                arrived(gw3_rx.at[j], gw_s.at[2, i], gw_r.at[2, j])
            gw4_rx[member] = jnp.sum(gw3_rx[...], axis=0)
            for i, j in enumerate(mpeers):
                send(gw4_rx.at[member], gw4_rx.at[member], gw_s.at[3, i], gw_r.at[3, member], device(j // 2, y, z, j % 2))
        else:
            for i, j in enumerate(mpeers):
                arrived(gw4_rx.at[j], gw_s.at[3, i], gw_r.at[3, j])
            gw5_rx[z] = gw4_rx[...]
            for i, j in enumerate(zpeers):
                send(gw5_rx.at[z], gw5_rx.at[z], gw_s.at[4, i], gw_r.at[4, z], device(x, y, j, k))

    for o in range(GROUP):
        px, pz, p, dev = peer(o)
        if o == 0:
            grads = grad_tx[...]
        else:
            arrived(grad_rx.at[p], grad_s.at[o], grad_r.at[p])
            grads = grad_rx[p]
        for c in range(ZH):
            pair, cols = live_tiles(p, c)
            both = jnp.dot(grads, pair, preferred_element_type=F32)
            for s in range(SLOTS):
                i = c * GROUP * SLOTS + o * SLOTS + s
                chain[i] = both[:, s * TILE:(s + 1) * TILE] + chain[prev_sm[i]]
        if o in (4, 6):
            weight_round(o // 2 - 2)

    def block(c, yy, half):
        return chain[last_sm[c * 2 * NY + yy * 2 + half]]

    def send_half(j):
        yy = yp(j)
        for c in range(ZH):
            sib_tx[yy, c] = block(c, yy, 1 - k).astype(BF16)
        send(sib_tx.at[yy], sib_rx.at[yy], sib_s.at[j % NY], sib_r.at[yy], sibling)

    def both_cores(yy, c):
        return block(c, yy, k) + sib_rx[yy, c].astype(F32)

    def reduce_step(s, target, tx, rx, ssem, rsem, dev):
        arrived(sib_rx.at[target], sib_s.at[0], sib_r.at[target])
        for c in (zothers[2], zothers[1], zothers[3], zh):
            value = both_cores(target, c)
            if s > 0:
                arrived(rx.at[s - 1, c], ssem.at[s - 1, c], rsem.at[s - 1, c])
                value += rx[s - 1, c].astype(F32)
            tx[s, c] = value.astype(BF16)
            send(tx.at[s, c], rx.at[s, c], ssem.at[s, c], rsem.at[s, c], dev)

    for s, halves in enumerate(((4, 3), (-3, 2), (-2, 1), (-1, 0))):
        for j in halves:
            send_half(j)
        reduce_step(s, yp(4 - s), plus_tx, plus_rx, plus_s, plus_r, up)
        if s < 3:
            reduce_step(s, yp(s - 3), minus_tx, minus_rx, minus_s, minus_r, down)
        if s < 2:
            weight_round(s + 2)

    arrived(sib_rx.at[y], sib_s.at[0], sib_r.at[y])
    for i in (2, 1, 3, 0):
        j = zothers[i]
        arrived(plus_rx.at[3, j], plus_s.at[3, j], plus_r.at[3, j])
        arrived(minus_rx.at[2, j], minus_s.at[2, j], minus_r.at[2, j])
        value = both_cores(y, j) + plus_rx[3, j].astype(F32) + minus_rx[2, j].astype(F32)
        zred_tx[i] = value.astype(BF16)
        if i > 0:
            send(zred_tx.at[i], zred_rx.at[zh], zred_s.at[i], zred_r.at[zh], partner(j))

    @pl.when(xl == k)
    def _():
        zred_rx[zh] = zred_tx[0]

    @pl.when(xl != k)
    def _():
        copy(zred_tx.at[0], zred_rx.at[zh], zred_s.at[0], zred_r.at[zh], partner(zh)).start()

    for i, j in enumerate(zpeers):
        arrived(gw5_rx.at[j], gw_s.at[4, i], gw_r.at[4, j])
    scale = 1.0 / 256.0
    for i in range(NZ):
        for j in range(GROUP):
            r0, c0 = i * 32 + (j % 4) * 8, (j // 4) * 128
            gw_ref[r0:r0 + 8, c0:c0 + 128] = gw5_rx[i, j] * scale

    for i in range(1, ZH):
        arrived(zred_rx.at[zothers[i]], zred_s.at[i], zred_r.at[zothers[i]])

    @pl.when(xl != k)
    def _():
        arrived(zred_rx.at[zh], zred_s.at[0], zred_r.at[zh])

    gf_ref[...] = jnp.sum(zred_rx[...].astype(F32), axis=0).T.astype(BF16)

    @pl.when(xl != k)
    def _():
        copy(zred_tx.at[0], zred_rx.at[zh], zred_s.at[0], zred_r.at[zh], partner(zh)).wait_send()
        copy(feat_ref, feats.at[xl, y, zh], agz_s.at[0], agz_r.at[zh], partner(zh)).wait_send()

    for c in sent:
        c.wait_send()


def finish(out_in, gf_in, gw_in, out_ref, gf_ref, gw_ref):
    out_ref[...] = out_in[...]
    gf_ref[...] = gf_in[...]
    gw_ref[...] = gw_in[...]


def body(features, weight, cotangent, tile_values, tile_cols, tile_counts):
    cols = tile_cols.reshape(32, SLOTS).T
    counts = tile_counts.reshape(1, 32)
    tiles = tile_values.reshape(2, ZH, 2, 2, SLOTS, TILE, TILE)
    dma, vmem = pltpu.SemaphoreType.DMA, pltpu.VMEM
    spec = pl.BlockSpec(memory_space=pltpu.VMEM)
    block = (D, TILE)
    results = pl.pallas_call(
        kernel,
        out_shape=(
            jax.ShapeDtypeStruct((TILE, D), BF16),
            jax.ShapeDtypeStruct((TILE, D), BF16),
            jax.ShapeDtypeStruct((D, D), F32),
        ),
        in_specs=[spec] * 5 + [pl.BlockSpec(memory_space=pl.ANY)],
        out_specs=(spec,) * 3,
        scratch_shapes=[
            vmem((GROUP, ZH, SLOTS, TILE, TILE), BF16),
            vmem((8, 128), jnp.int32),
            vmem((GROUP, 8, 128), jnp.int32),
            pltpu.SMEM((GROUP, 8, 128), jnp.int32),
            pltpu.SMEM((TERMS,), jnp.int32),
            pltpu.SMEM((ZH * 2 * NY,), jnp.int32),
            vmem((2, NY, ZH, TILE, D), BF16),
            vmem((GROUP, TILE, D), BF16),
            vmem((GROUP, TILE, D), BF16),
            vmem(block, BF16),
            vmem((GROUP,) + block, BF16),
            vmem((TERMS + 1,) + block, F32),
            vmem((NY, ZH) + block, BF16),
            vmem((NY, ZH) + block, BF16),
            vmem((4, ZH) + block, BF16),
            vmem((4, ZH) + block, BF16),
            vmem((3, ZH) + block, BF16),
            vmem((3, ZH) + block, BF16),
            vmem((ZH,) + block, BF16),
            vmem((ZH,) + block, BF16),
            vmem((NZ, GROUP, 8, 128), F32),
            vmem((NZ, GROUP, 8, 128), F32),
            vmem((GROUP, 8, 128), F32),
            vmem((GROUP, 8, 128), F32),
            vmem((NY, 8, 128), F32),
            vmem((GROUP, 8, 128), F32),
            vmem((NZ, GROUP, 8, 128), F32),
            dma((2,)),
            dma((GROUP, ZH)), dma((GROUP, ZH)),
            dma((GROUP,)), dma((GROUP,)),
            dma((ZH,)), dma((ZH,)),
            dma((4, ZH)), dma((4, ZH)),
            dma((3, ZH)), dma((3, ZH)),
            dma((NY,)), dma((NY,)),
            dma((GROUP,)), dma((GROUP,)),
            dma((GROUP,)), dma((GROUP,)),
            dma((NY,)), dma((NY,)),
            dma((4, ZH)), dma((4, ZH)),
            dma((3, ZH)), dma((3, ZH)),
            dma((ZH,)), dma((ZH,)),
            dma((5, 8)), dma((5, 8)),
        ],
        compiler_params=pltpu.CompilerParams(
            collective_id=0, has_side_effects=True, vmem_limit_bytes=56 * 1024 * 1024
        ),
    )(features, weight, cotangent, cols, counts, tiles)
    return pl.pallas_call(
        finish,
        out_shape=tuple(jax.ShapeDtypeStruct(r.shape, r.dtype) for r in results),
        in_specs=[spec] * 3,
        out_specs=(spec,) * 3,
        compiler_params=pltpu.CompilerParams(vmem_limit_bytes=63 * 1024 * 1024),
    )(*results)


def solution(mesh):
    return jax.shard_map(
        body,
        mesh=mesh,
        in_specs=(
            P(("section", "rep"), None),
            P(),
            P(("section", "rep"), None),
            P("section", "rep", None, None, None, None),
            P("section", "rep", None, None),
            P("section", "rep", None),
        ),
        out_specs=(P(("section", "rep"), None), P(("section", "rep"), None), P()),
        check_vma=False,
    )
```

```python
import jax
import jax.numpy as jnp
from jax import lax
from jax.experimental import pallas as pl
from jax.experimental.pallas import tpu as pltpu
from jax.sharding import PartitionSpec as P

MESH = pl.DeviceIdType.MESH
F32 = jnp.float32
BF16 = jnp.bfloat16
NX, NY, NZ = 4, 8, 8
ZH = NZ // 2
GROUP = 2 * NX
SLOTS = 2
TILE = 128
D = 256
TERMS = ZH * GROUP * SLOTS
ORDER = (0, 4, 2, 1, 6, 5, 3, 7)
ZERO = TERMS


def device(x, y, z, k):
    return ((x // 2) * (2 * NZ) + z * 2 + k, y * 2 + x % 2)


def kernel(
    feat_ref, weight_ref, cot_ref, cols_ref, counts_ref, tiles_ref,
    out_ref, gf_ref, gw_ref,
    tiles_rx, meta_tx, meta_rx, meta_sm, prev_sm, last_sm,
    feats, part_tx, part_pass, part_rx, grad_tx, grad_rx, chain,
    sib_tx, sib_rx, plus_tx, plus_rx, minus_tx, minus_rx, zred_tx, zred_rx,
    gw1_tx, gw1_rx, gw2_tx, gw2_rx, gw3_rx, gw4_rx, gw5_rx,
    local_sem, pass_r, tile_s, tile_r, meta_s, meta_r, agz_s, agz_r,
    agp_s, agp_r, agm_s, agm_r, agd_s, agd_r, part_s, part_r, grad_s, grad_r,
    sib_s, sib_r, plus_s, plus_r, minus_s, minus_r, zred_s, zred_r,
    gw_s, gw_r,
):
    section, rep = lax.axis_index("section"), lax.axis_index("rep")
    xh, z, k = section // (2 * NZ), (section // 2) % NZ, section % 2
    y, xl = rep // 2, rep % 2
    x = 2 * xh + xl
    zp, zh = z % 2, z // 2
    member = x * 2 + k
    turn = 1 - 2 * k
    zpair = (z + turn * (1 - 2 * zp) + NZ) % NZ
    mine = x * 2 + zp
    sibling = device(x, y, z, 1 - k)

    def partner(j):
        return device(2 * xh + k, y, j * 2 + zp, xl)

    def yp(j):
        return (y + turn * j + 2 * NY) % NY

    def group(o):
        h = o // 2
        px = (x + turn * (h + (h // 2) * (1 - 2 * (h % 2))) + 2 * NX) % NX
        pz = (zp + o % 2) % 2
        return px, pz, px * 2 + pz

    def peer(o):
        px, pz, p = group(o)
        return px, pz, p, device(px, y, zpair if o % 2 else z, k)

    def copy(src, dst, send, recv, dev):
        return pltpu.make_async_remote_copy(
            src_ref=src, dst_ref=dst, send_sem=send, recv_sem=recv,
            device_id=dev, device_id_type=MESH,
        )

    sent = []

    def send(src, dst, ssem, rsem, dev):
        c = copy(src, dst, ssem, rsem, dev)
        c.start()
        sent.append(c)

    def arrived(dst, ssem, rsem):
        copy(dst, dst, ssem, rsem, sibling).wait_recv()

    ypeers = [(y + i) % NY for i in range(1, NY)]
    zpeers = [(z + i) % NZ for i in range(1, NZ)]
    mpeers = [(member + i) % GROUP for i in range(1, GROUP)]

    own_tiles = pltpu.make_async_copy(
        tiles_ref.at[x // 2, :, zp, x % 2], tiles_rx.at[mine], local_sem.at[0]
    )
    own_tiles.start()

    barrier = pltpu.get_barrier_semaphore()
    everyone = (
        [device(x, j, z, k) for j in ypeers]
        + [device(x, y, j, k) for j in zpeers]
        + [device(j // 2, y, z, j % 2) for j in mpeers]
        + [peer(o)[3] for o in (3, 5, 7)]
        + [partner((zh + i) % ZH) for i in range(1, ZH)]
    )
    for dev in everyone:
        pl.semaphore_signal(barrier, inc=1, device_id=dev, device_id_type=MESH)
    pl.semaphore_wait(barrier, len(everyone))

    @pl.when(xl == k)
    def _():
        feats[k, y, zh] = feat_ref[...]

    @pl.when(xl != k)
    def _():
        copy(feat_ref, feats.at[xl, y, zh], agz_s.at[0], agz_r.at[zh], partner(zh)).start()

    zothers = [(zh + i) % ZH for i in range(ZH)]
    for i in range(1, ZH):
        send(feat_ref, feats.at[xl, y, zh], agz_s.at[i], agz_r.at[zh], partner(zothers[i]))

    dead = lax.broadcasted_iota(jnp.int32, (SLOTS, 32), 0) >= counts_ref[...]
    meta_tx[...] = jnp.zeros_like(meta_tx)
    meta_tx[0:SLOTS, 0:32] = cols_ref[...] + jnp.where(dead, 2 * NY, 0)
    for o in range(1, GROUP):
        px, pz, p, dev = peer(o)
        send(meta_tx, meta_rx.at[mine], meta_s.at[o], meta_r.at[mine], dev)
    meta_rx[mine] = meta_tx[...]

    def send_tiles(c):
        for o in range(1, GROUP):
            px, pz, p, dev = peer(o)
            send(
                tiles_ref.at[px // 2, c, pz, px % 2], tiles_rx.at[mine, c],
                tile_s.at[o, c], tile_r.at[mine, c], dev,
            )

    def column_section(c):
        return (x // 2) * (2 * NZ) + c * 4 + zp * 2 + x % 2

    def column_table():
        for o in range(1, GROUP):
            p = peer(o)[2]
            arrived(meta_rx.at[p], meta_s.at[o], meta_r.at[p])
        to_scalar = pltpu.make_async_copy(meta_rx, meta_sm, local_sem.at[1])
        to_scalar.start()
        to_scalar.wait()

        @pl.loop(0, ZH * 2 * NY)
        def _(q):
            last_sm[q] = ZERO

        for n, o in enumerate(ORDER):
            p = group(o)[2]

            @pl.loop(0, ZH * SLOTS)
            def _(t):
                c, s = t // SLOTS, t % SLOTS
                i = c * (GROUP * SLOTS) + n * SLOTS + s
                col = meta_sm[p, s, column_section(c)] % (2 * NY)
                prev_sm[i] = last_sm[c * 2 * NY + col]
                for q in range(2 * NY):
                    last_sm[c * 2 * NY + q] = jnp.where(col == q, i, last_sm[c * 2 * NY + q])

        chain[ZERO] = jnp.zeros((D, TILE), F32)

    up, down = device(x, yp(1), z, k), device(x, yp(-1), z, k)

    def gather_plus(s, i):
        c, j = yp(-s), zothers[i]
        send(feats.at[k, c, j], feats.at[k, c, j], agp_s.at[s, i], agp_r.at[s, i], up)

    def gather_minus(s, i):
        c, j = yp(s), zothers[i]
        send(feats.at[k, c, j], feats.at[k, c, j], agm_s.at[s, i], agm_r.at[s, i], down)

    def gather_sibling(j):
        c = yp(j)
        send(feats.at[k, c], feats.at[k, c], agd_s.at[j % NY], agd_r.at[c], sibling)

    send_tiles(0)
    for i in range(ZH):
        j = zothers[i]
        if i == 0:
            @pl.when(xl != k)
            def _():
                arrived(feats.at[k, y, zh], agz_s.at[0], agz_r.at[zh])
        else:
            arrived(feats.at[k, y, j], agz_s.at[i], agz_r.at[j])
        gather_plus(0, i)
        gather_minus(0, i)
    gather_sibling(0)
    send_tiles(1)
    for s in range(4):
        if s == 3:
            column_table()
        for i in range(ZH):
            arrived(feats.at[k, yp(-s - 1), zothers[i]], agp_s.at[s, i], agp_r.at[s, i])
            if s < 3:
                gather_plus(s + 1, i)
                arrived(feats.at[k, yp(s + 1), zothers[i]], agm_s.at[s, i], agm_r.at[s, i])
                if s < 2:
                    gather_minus(s + 1, i)
        gather_sibling(-s - 1)
        if s < 3:
            gather_sibling(s + 1)
        if s < 2:
            send_tiles(s + 2)

    for j in range(NY):
        c = (y + j) % NY
        arrived(feats.at[1 - k, c], agd_s.at[0], agd_r.at[c])

    def live_tiles(p, c):
        tiles, codes = [], []
        for s in range(SLOTS):
            code = meta_sm[p, s, column_section(c)]
            tile = tiles_rx[p, c, s]
            tiles.append(jnp.where(code < 2 * NY, tile, jnp.zeros_like(tile)))
            codes.append(code % (2 * NY))
        return jnp.concatenate(tiles, axis=1), codes

    total = None
    for o in (6, 7, 4, 5, 1, 2, 3, 0):
        px, pz, p, dev = peer(o)
        if o == 0:
            own_tiles.wait()
        else:
            for c in range(ZH):
                arrived(tiles_rx.at[p, c], tile_s.at[o, c], tile_r.at[p, c])
        acc = jnp.zeros((TILE, D), F32)
        for c in range(ZH):
            pair, cols = live_tiles(p, c)
            rows = jnp.concatenate([feats[col % 2, col // 2, c] for col in cols], axis=0)
            acc += jnp.dot(pair, rows, preferred_element_type=F32)
        if o == 0:
            total = acc
        else:
            if o in (2, 3):
                arrived(part_pass.at[o - 2], part_s.at[o], pass_r.at[o - 2])
                acc += part_pass[o - 2].astype(F32)
            part_tx[o] = acc.astype(BF16)
            dst, rsem = part_rx.at[mine], part_r.at[mine]
            if o >= 6:
                dst, rsem, dev = part_pass.at[o - 6], pass_r.at[o - 6], peer(2)[3]
            send(part_tx.at[o], dst, part_s.at[o], rsem, dev)
    for o in range(1, 6):
        p = peer(o)[2]
        arrived(part_rx.at[p], part_s.at[o], part_r.at[p])
        total += part_rx[p].astype(F32)

    aggregated = total.astype(BF16)
    weight = weight_ref[...]
    pre = jnp.dot(aggregated, weight, preferred_element_type=F32)
    sig = lax.logistic(pre)
    out_ref[...] = (pre * sig).astype(BF16)
    grad_pre = (cot_ref[...].astype(F32) * sig * (1.0 + pre * (1.0 - sig))).astype(BF16)
    grad_tx[...] = lax.dot_general(
        weight, grad_pre, (((1,), (1,)), ((), ())), preferred_element_type=F32
    ).astype(BF16)
    for n, o in enumerate((4, 2, 1)):
        send(grad_tx, grad_rx.at[mine], grad_s.at[n], grad_r.at[mine], peer(o)[3])

    def pass_grads(o, n, targets):
        p = group(o)[2]
        arrived(grad_rx.at[p], grad_s.at[n], grad_r.at[p])
        for i, t in enumerate(targets):
            send(grad_rx.at[p], grad_rx.at[p], grad_s.at[n + i], grad_r.at[p], peer(t)[3])

    terms = lax.dot_general(
        aggregated, grad_pre, (((0,), (0,)), ((), ())), preferred_element_type=F32
    )
    for i in range(NZ):
        for j in range(GROUP):
            r0, c0 = i * 32 + (j % 4) * 8, (j // 4) * 128
            gw1_tx[i, j] = terms[r0:r0 + 8, c0:c0 + 128]
    for i, j in enumerate(zpeers):
        send(gw1_tx.at[j], gw1_rx.at[z], gw_s.at[0, i], gw_r.at[0, z], device(x, y, j, k))
    gw1_rx[z] = gw1_tx[z]

    def weight_round(s):
        if s == 0:
            for i, j in enumerate(zpeers):
                arrived(gw1_rx.at[j], gw_s.at[0, i], gw_r.at[0, j])
            gw2_tx[...] = jnp.sum(gw1_rx[...], axis=0)
            for i, j in enumerate(mpeers):
                send(gw2_tx.at[j], gw2_rx.at[member], gw_s.at[1, i], gw_r.at[1, member], device(j // 2, y, z, j % 2))
            gw2_rx[member] = gw2_tx[member]
        elif s == 1:
            for i, j in enumerate(mpeers):
                arrived(gw2_rx.at[j], gw_s.at[1, i], gw_r.at[1, j])
            gw3_rx[y] = jnp.sum(gw2_rx[...], axis=0)
            for i, j in enumerate(ypeers):
                send(gw3_rx.at[y], gw3_rx.at[y], gw_s.at[2, i], gw_r.at[2, y], device(x, j, z, k))
        elif s == 2:
            for i, j in enumerate(ypeers):
                arrived(gw3_rx.at[j], gw_s.at[2, i], gw_r.at[2, j])
            gw4_rx[member] = jnp.sum(gw3_rx[...], axis=0)
            for i, j in enumerate(mpeers):
                send(gw4_rx.at[member], gw4_rx.at[member], gw_s.at[3, i], gw_r.at[3, member], device(j // 2, y, z, j % 2))
        else:
            for i, j in enumerate(mpeers):
                arrived(gw4_rx.at[j], gw_s.at[3, i], gw_r.at[3, j])
            gw5_rx[z] = gw4_rx[...]
            for i, j in enumerate(zpeers):
                send(gw5_rx.at[z], gw5_rx.at[z], gw_s.at[4, i], gw_r.at[4, z], device(x, y, j, k))

    for n, o in enumerate(ORDER):
        p = group(o)[2]
        if n == 1:
            pass_grads(4, 3, (2, 1))
            pass_grads(2, 5, (1,))
        elif n == 3:
            pass_grads(6, 6, (1,))
            arrived(grad_rx.at[p], grad_s.at[0], grad_r.at[p])
        elif o in (5, 3, 7):
            arrived(grad_rx.at[p], grad_s.at[0], grad_r.at[p])
        grads = grad_rx[p] if o else grad_tx[...]
        for c in range(ZH):
            pair, cols = live_tiles(p, c)
            both = jnp.dot(grads, pair, preferred_element_type=F32)
            for s in range(SLOTS):
                i = c * GROUP * SLOTS + n * SLOTS + s
                chain[i] = both[:, s * TILE:(s + 1) * TILE] + chain[prev_sm[i]]
        if n in (3, 5):
            weight_round((n - 3) // 2)

    def block(c, yy, half):
        return chain[last_sm[c * 2 * NY + yy * 2 + half]]

    def send_half(j):
        yy = yp(j)
        for c in range(ZH):
            sib_tx[yy, c] = block(c, yy, 1 - k).astype(BF16)
        send(sib_tx.at[yy], sib_rx.at[yy], sib_s.at[j % NY], sib_r.at[yy], sibling)

    def both_cores(yy, c):
        return block(c, yy, k) + sib_rx[yy, c].astype(F32)

    def reduce_step(s, target, tx, rx, ssem, rsem, dev):
        arrived(sib_rx.at[target], sib_s.at[0], sib_r.at[target])
        for c in (zothers[2], zothers[1], zothers[3], zh):
            value = both_cores(target, c)
            if s > 0:
                arrived(rx.at[s - 1, c], ssem.at[s - 1, c], rsem.at[s - 1, c])
                value += rx[s - 1, c].astype(F32)
            tx[s, c] = value.astype(BF16)
            send(tx.at[s, c], rx.at[s, c], ssem.at[s, c], rsem.at[s, c], dev)

    for s, halves in enumerate(((4, 3), (-3, 2), (-2, 1), (-1, 0))):
        for j in halves:
            send_half(j)
        reduce_step(s, yp(4 - s), plus_tx, plus_rx, plus_s, plus_r, up)
        if s < 3:
            reduce_step(s, yp(s - 3), minus_tx, minus_rx, minus_s, minus_r, down)
        if s < 2:
            weight_round(s + 2)

    arrived(sib_rx.at[y], sib_s.at[0], sib_r.at[y])
    for i in (2, 1, 3, 0):
        j = zothers[i]
        arrived(plus_rx.at[3, j], plus_s.at[3, j], plus_r.at[3, j])
        arrived(minus_rx.at[2, j], minus_s.at[2, j], minus_r.at[2, j])
        value = both_cores(y, j) + plus_rx[3, j].astype(F32) + minus_rx[2, j].astype(F32)
        zred_tx[i] = value.astype(BF16)
        if i > 0:
            send(zred_tx.at[i], zred_rx.at[zh], zred_s.at[i], zred_r.at[zh], partner(j))

    @pl.when(xl == k)
    def _():
        zred_rx[zh] = zred_tx[0]

    @pl.when(xl != k)
    def _():
        copy(zred_tx.at[0], zred_rx.at[zh], zred_s.at[0], zred_r.at[zh], partner(zh)).start()

    for i, j in enumerate(zpeers):
        arrived(gw5_rx.at[j], gw_s.at[4, i], gw_r.at[4, j])
    scale = 1.0 / 256.0
    for i in range(NZ):
        for j in range(GROUP):
            r0, c0 = i * 32 + (j % 4) * 8, (j // 4) * 128
            gw_ref[r0:r0 + 8, c0:c0 + 128] = gw5_rx[i, j] * scale

    for i in range(1, ZH):
        arrived(zred_rx.at[zothers[i]], zred_s.at[i], zred_r.at[zothers[i]])

    @pl.when(xl != k)
    def _():
        arrived(zred_rx.at[zh], zred_s.at[0], zred_r.at[zh])

    gf_ref[...] = jnp.sum(zred_rx[...].astype(F32), axis=0).T.astype(BF16)

    @pl.when(xl != k)
    def _():
        copy(zred_tx.at[0], zred_rx.at[zh], zred_s.at[0], zred_r.at[zh], partner(zh)).wait_send()
        copy(feat_ref, feats.at[xl, y, zh], agz_s.at[0], agz_r.at[zh], partner(zh)).wait_send()

    for c in sent:
        c.wait_send()


def finish(out_in, gf_in, gw_in, out_ref, gf_ref, gw_ref):
    out_ref[...] = out_in[...]
    gf_ref[...] = gf_in[...]
    gw_ref[...] = gw_in[...]


def body(features, weight, cotangent, tile_values, tile_cols, tile_counts):
    cols = tile_cols.reshape(32, SLOTS).T
    counts = tile_counts.reshape(1, 32)
    tiles = tile_values.reshape(2, ZH, 2, 2, SLOTS, TILE, TILE)
    dma, vmem = pltpu.SemaphoreType.DMA, pltpu.VMEM
    spec = pl.BlockSpec(memory_space=pltpu.VMEM)
    block = (D, TILE)
    results = pl.pallas_call(
        kernel,
        out_shape=(
            jax.ShapeDtypeStruct((TILE, D), BF16),
            jax.ShapeDtypeStruct((TILE, D), BF16),
            jax.ShapeDtypeStruct((D, D), F32),
        ),
        in_specs=[spec] * 5 + [pl.BlockSpec(memory_space=pl.ANY)],
        out_specs=(spec,) * 3,
        scratch_shapes=[
            vmem((GROUP, ZH, SLOTS, TILE, TILE), BF16),
            vmem((8, 128), jnp.int32),
            vmem((GROUP, 8, 128), jnp.int32),
            pltpu.SMEM((GROUP, 8, 128), jnp.int32),
            pltpu.SMEM((TERMS,), jnp.int32),
            pltpu.SMEM((ZH * 2 * NY,), jnp.int32),
            vmem((2, NY, ZH, TILE, D), BF16),
            vmem((GROUP, TILE, D), BF16),
            vmem((2, TILE, D), BF16),
            vmem((GROUP, TILE, D), BF16),
            vmem(block, BF16),
            vmem((GROUP,) + block, BF16),
            vmem((TERMS + 1,) + block, F32),
            vmem((NY, ZH) + block, BF16),
            vmem((NY, ZH) + block, BF16),
            vmem((4, ZH) + block, BF16),
            vmem((4, ZH) + block, BF16),
            vmem((3, ZH) + block, BF16),
            vmem((3, ZH) + block, BF16),
            vmem((ZH,) + block, BF16),
            vmem((ZH,) + block, BF16),
            vmem((NZ, GROUP, 8, 128), F32),
            vmem((NZ, GROUP, 8, 128), F32),
            vmem((GROUP, 8, 128), F32),
            vmem((GROUP, 8, 128), F32),
            vmem((NY, 8, 128), F32),
            vmem((GROUP, 8, 128), F32),
            vmem((NZ, GROUP, 8, 128), F32),
            dma((2,)), dma((2,)),
            dma((GROUP, ZH)), dma((GROUP, ZH)),
            dma((GROUP,)), dma((GROUP,)),
            dma((ZH,)), dma((ZH,)),
            dma((4, ZH)), dma((4, ZH)),
            dma((3, ZH)), dma((3, ZH)),
            dma((NY,)), dma((NY,)),
            dma((GROUP,)), dma((GROUP,)),
            dma((GROUP,)), dma((GROUP,)),
            dma((NY,)), dma((NY,)),
            dma((4, ZH)), dma((4, ZH)),
            dma((3, ZH)), dma((3, ZH)),
            dma((ZH,)), dma((ZH,)),
            dma((5, 8)), dma((5, 8)),
        ],
        compiler_params=pltpu.CompilerParams(
            collective_id=0, has_side_effects=True, vmem_limit_bytes=56 * 1024 * 1024
        ),
    )(features, weight, cotangent, cols, counts, tiles)
    return pl.pallas_call(
        finish,
        out_shape=tuple(jax.ShapeDtypeStruct(r.shape, r.dtype) for r in results),
        in_specs=[spec] * 3,
        out_specs=(spec,) * 3,
        compiler_params=pltpu.CompilerParams(vmem_limit_bytes=63 * 1024 * 1024),
    )(*results)


def solution(mesh):
    return jax.shard_map(
        body,
        mesh=mesh,
        in_specs=(
            P(("section", "rep"), None),
            P(),
            P(("section", "rep"), None),
            P("section", "rep", None, None, None, None),
            P("section", "rep", None, None),
            P("section", "rep", None),
        ),
        out_specs=(P(("section", "rep"), None), P(("section", "rep"), None), P()),
        check_vma=False,
    )
```

```python
import jax
import jax.numpy as jnp
from jax import lax
from jax.experimental import pallas as pl
from jax.experimental.pallas import tpu as pltpu
from jax.sharding import PartitionSpec as P

MESH = pl.DeviceIdType.MESH
F32 = jnp.float32
BF16 = jnp.bfloat16
NX, NY, NZ = 4, 8, 8
ZH = NZ // 2
GROUP = 2 * NX
SLOTS = 2
TILE = 128
D = 256
TERMS = ZH * GROUP * SLOTS
ORDER = (0, 4, 2, 1, 6, 5, 3, 7)
ZERO = TERMS


def device(x, y, z, k):
    return ((x // 2) * (2 * NZ) + z * 2 + k, y * 2 + x % 2)


def kernel(
    feat_ref, weight_ref, cot_ref, cols_ref, counts_ref, tiles_ref,
    out_ref, gf_ref, gw_ref,
    tiles_rx, meta_tx, meta_rx, meta_sm, prev_sm, last_sm,
    feats, part_tx, part_pass, part_rx, grad_tx, grad_rx, chain,
    sib_tx, sib_rx, plus_tx, plus_rx, minus_tx, minus_rx, zred_tx, zred_rx,
    gw1_tx, gw1_rx, gw2_tx, gw2_rx, gw3_rx, gw4_rx, gw5_rx,
    local_sem, pass_r, tile_s, tile_r, meta_s, meta_r, agz_s, agz_r,
    agp_s, agp_r, agm_s, agm_r, agd_s, agd_r, part_s, part_r, grad_s, grad_r,
    sib_s, sib_r, plus_s, plus_r, minus_s, minus_r, zred_s, zred_r,
    gw_s, gw_r,
):
    section, rep = lax.axis_index("section"), lax.axis_index("rep")
    xh, z, k = section // (2 * NZ), (section // 2) % NZ, section % 2
    y, xl = rep // 2, rep % 2
    x = 2 * xh + xl
    zp, zh = z % 2, z // 2
    member = x * 2 + k
    turn = 1 - 2 * k
    zpair = (z + turn * (1 - 2 * zp) + NZ) % NZ
    mine = x * 2 + zp
    sibling = device(x, y, z, 1 - k)

    def partner(j):
        return device(2 * xh + k, y, j * 2 + zp, xl)

    def yp(j):
        return (y + turn * j + 2 * NY) % NY

    def group(o):
        h = o // 2
        px = (x + turn * (h + (h // 2) * (1 - 2 * (h % 2))) + 2 * NX) % NX
        pz = (zp + o % 2) % 2
        return px, pz, px * 2 + pz

    def peer(o):
        px, pz, p = group(o)
        return px, pz, p, device(px, y, zpair if o % 2 else z, k)

    def copy(src, dst, send, recv, dev):
        return pltpu.make_async_remote_copy(
            src_ref=src, dst_ref=dst, send_sem=send, recv_sem=recv,
            device_id=dev, device_id_type=MESH,
        )

    sent = []

    def send(src, dst, ssem, rsem, dev):
        c = copy(src, dst, ssem, rsem, dev)
        c.start()
        sent.append(c)

    def arrived(dst, ssem, rsem):
        copy(dst, dst, ssem, rsem, sibling).wait_recv()

    ypeers = [(y + i) % NY for i in range(1, NY)]
    zpeers = [(z + i) % NZ for i in range(1, NZ)]
    mpeers = [(member + i) % GROUP for i in range(1, GROUP)]

    own_tiles = pltpu.make_async_copy(
        tiles_ref.at[x // 2, :, zp, x % 2], tiles_rx.at[mine], local_sem.at[0]
    )
    own_tiles.start()

    barrier = pltpu.get_barrier_semaphore()
    everyone = (
        [device(x, j, z, k) for j in ypeers]
        + [device(x, y, j, k) for j in zpeers]
        + [device(j // 2, y, z, j % 2) for j in mpeers]
        + [peer(o)[3] for o in (3, 5, 7)]
        + [partner((zh + i) % ZH) for i in range(1, ZH)]
    )
    for dev in everyone:
        pl.semaphore_signal(barrier, inc=1, device_id=dev, device_id_type=MESH)
    pl.semaphore_wait(barrier, len(everyone))

    @pl.when(xl == k)
    def _():
        feats[k, y, zh] = feat_ref[...]

    @pl.when(xl != k)
    def _():
        copy(feat_ref, feats.at[xl, y, zh], agz_s.at[0], agz_r.at[zh], partner(zh)).start()

    zothers = [(zh + i) % ZH for i in range(ZH)]
    for i in range(1, ZH):
        send(feat_ref, feats.at[xl, y, zh], agz_s.at[i], agz_r.at[zh], partner(zothers[i]))

    dead = lax.broadcasted_iota(jnp.int32, (SLOTS, 32), 0) >= counts_ref[...]
    meta_tx[...] = jnp.zeros_like(meta_tx)
    meta_tx[0:SLOTS, 0:32] = cols_ref[...] + jnp.where(dead, 2 * NY, 0)
    for o in range(1, GROUP):
        px, pz, p, dev = peer(o)
        send(meta_tx, meta_rx.at[mine], meta_s.at[o], meta_r.at[mine], dev)
    meta_rx[mine] = meta_tx[...]

    def send_tiles(c):
        for o in (6, 7, 4, 5, 1, 2, 3):
            px, pz, p, dev = peer(o)
            send(
                tiles_ref.at[px // 2, c, pz, px % 2], tiles_rx.at[mine, c],
                tile_s.at[o, c], tile_r.at[mine, c], dev,
            )

    def column_section(c):
        return (x // 2) * (2 * NZ) + c * 4 + zp * 2 + x % 2

    def column_table():
        for o in range(1, GROUP):
            p = peer(o)[2]
            arrived(meta_rx.at[p], meta_s.at[o], meta_r.at[p])
        to_scalar = pltpu.make_async_copy(meta_rx, meta_sm, local_sem.at[1])
        to_scalar.start()
        to_scalar.wait()

        @pl.loop(0, ZH * 2 * NY)
        def _(q):
            last_sm[q] = ZERO

        for n, o in enumerate(ORDER):
            p = group(o)[2]

            @pl.loop(0, ZH * SLOTS)
            def _(t):
                c, s = t // SLOTS, t % SLOTS
                i = c * (GROUP * SLOTS) + n * SLOTS + s
                col = meta_sm[p, s, column_section(c)] % (2 * NY)
                prev_sm[i] = last_sm[c * 2 * NY + col]
                for q in range(2 * NY):
                    last_sm[c * 2 * NY + q] = jnp.where(col == q, i, last_sm[c * 2 * NY + q])

        chain[ZERO] = jnp.zeros((D, TILE), F32)

    up, down = device(x, yp(1), z, k), device(x, yp(-1), z, k)

    def gather_plus(s, i):
        c, j = yp(-s), zothers[i]
        send(feats.at[k, c, j], feats.at[k, c, j], agp_s.at[s, i], agp_r.at[s, i], up)

    def gather_minus(s, i):
        c, j = yp(s), zothers[i]
        send(feats.at[k, c, j], feats.at[k, c, j], agm_s.at[s, i], agm_r.at[s, i], down)

    def gather_sibling(j):
        c = yp(j)
        send(feats.at[k, c], feats.at[k, c], agd_s.at[j % NY], agd_r.at[c], sibling)

    send_tiles(0)
    for i in range(ZH):
        j = zothers[i]
        if i == 0:
            @pl.when(xl != k)
            def _():
                arrived(feats.at[k, y, zh], agz_s.at[0], agz_r.at[zh])
        else:
            arrived(feats.at[k, y, j], agz_s.at[i], agz_r.at[j])
        gather_plus(0, i)
        gather_minus(0, i)
    gather_sibling(0)
    send_tiles(1)
    for s in range(4):
        if s == 3:
            column_table()
        for i in range(ZH):
            arrived(feats.at[k, yp(-s - 1), zothers[i]], agp_s.at[s, i], agp_r.at[s, i])
            if s < 3:
                gather_plus(s + 1, i)
                arrived(feats.at[k, yp(s + 1), zothers[i]], agm_s.at[s, i], agm_r.at[s, i])
                if s < 2:
                    gather_minus(s + 1, i)
        gather_sibling(-s - 1)
        if s < 3:
            gather_sibling(s + 1)
        if s < 2:
            send_tiles(s + 2)

    for j in range(NY):
        c = (y + j) % NY
        arrived(feats.at[1 - k, c], agd_s.at[0], agd_r.at[c])

    def live_tiles(p, c):
        tiles, codes = [], []
        for s in range(SLOTS):
            code = meta_sm[p, s, column_section(c)]
            tile = tiles_rx[p, c, s]
            tiles.append(jnp.where(code < 2 * NY, tile, jnp.zeros_like(tile)))
            codes.append(code % (2 * NY))
        return jnp.concatenate(tiles, axis=1), codes

    total = None
    for o in (6, 7, 4, 5, 1, 2, 3, 0):
        px, pz, p, dev = peer(o)
        if o == 0:
            own_tiles.wait()
        else:
            for c in range(ZH):
                arrived(tiles_rx.at[p, c], tile_s.at[o, c], tile_r.at[p, c])
        acc = jnp.zeros((TILE, D), F32)
        for c in range(ZH):
            pair, cols = live_tiles(p, c)
            rows = jnp.concatenate([feats[col % 2, col // 2, c] for col in cols], axis=0)
            acc += jnp.dot(pair, rows, preferred_element_type=F32)
        if o == 0:
            total = acc
        else:
            if o in (2, 3):
                arrived(part_pass.at[o - 2], part_s.at[o], pass_r.at[o - 2])
                acc += part_pass[o - 2].astype(F32)
            part_tx[o] = acc.astype(BF16)
            dst, rsem = part_rx.at[mine], part_r.at[mine]
            if o >= 6:
                dst, rsem, dev = part_pass.at[o - 6], pass_r.at[o - 6], peer(2)[3]
            send(part_tx.at[o], dst, part_s.at[o], rsem, dev)
    for o in range(1, 6):
        p = peer(o)[2]
        arrived(part_rx.at[p], part_s.at[o], part_r.at[p])
        total += part_rx[p].astype(F32)

    aggregated = total.astype(BF16)
    weight = weight_ref[...]
    pre = jnp.dot(aggregated, weight, preferred_element_type=F32)
    sig = lax.logistic(pre)
    out_ref[...] = (pre * sig).astype(BF16)
    grad_pre = (cot_ref[...].astype(F32) * sig * (1.0 + pre * (1.0 - sig))).astype(BF16)
    grad_tx[...] = lax.dot_general(
        weight, grad_pre, (((1,), (1,)), ((), ())), preferred_element_type=F32
    ).astype(BF16)
    for n, o in enumerate((4, 2, 1)):
        send(grad_tx, grad_rx.at[mine], grad_s.at[n], grad_r.at[mine], peer(o)[3])

    def pass_grads(o, n, targets):
        p = group(o)[2]
        arrived(grad_rx.at[p], grad_s.at[n], grad_r.at[p])
        for i, t in enumerate(targets):
            send(grad_rx.at[p], grad_rx.at[p], grad_s.at[n + i], grad_r.at[p], peer(t)[3])

    terms = lax.dot_general(
        aggregated, grad_pre, (((0,), (0,)), ((), ())), preferred_element_type=F32
    )
    for i in range(NZ):
        for j in range(GROUP):
            r0, c0 = i * 32 + (j % 4) * 8, (j // 4) * 128
            gw1_tx[i, j] = terms[r0:r0 + 8, c0:c0 + 128]
    for i, j in enumerate(zpeers):
        send(gw1_tx.at[j], gw1_rx.at[z], gw_s.at[0, i], gw_r.at[0, z], device(x, y, j, k))
    gw1_rx[z] = gw1_tx[z]

    def weight_round(s):
        if s == 0:
            for i, j in enumerate(zpeers):
                arrived(gw1_rx.at[j], gw_s.at[0, i], gw_r.at[0, j])
            gw2_tx[...] = jnp.sum(gw1_rx[...], axis=0)
            for i, j in enumerate(mpeers):
                send(gw2_tx.at[j], gw2_rx.at[member], gw_s.at[1, i], gw_r.at[1, member], device(j // 2, y, z, j % 2))
            gw2_rx[member] = gw2_tx[member]
        elif s == 1:
            for i, j in enumerate(mpeers):
                arrived(gw2_rx.at[j], gw_s.at[1, i], gw_r.at[1, j])
            gw3_rx[y] = jnp.sum(gw2_rx[...], axis=0)
            for i, j in enumerate(ypeers):
                send(gw3_rx.at[y], gw3_rx.at[y], gw_s.at[2, i], gw_r.at[2, y], device(x, j, z, k))
        elif s == 2:
            for i, j in enumerate(ypeers):
                arrived(gw3_rx.at[j], gw_s.at[2, i], gw_r.at[2, j])
            gw4_rx[member] = jnp.sum(gw3_rx[...], axis=0)
            for i, j in enumerate(mpeers):
                send(gw4_rx.at[member], gw4_rx.at[member], gw_s.at[3, i], gw_r.at[3, member], device(j // 2, y, z, j % 2))
        else:
            for i, j in enumerate(mpeers):
                arrived(gw4_rx.at[j], gw_s.at[3, i], gw_r.at[3, j])
            gw5_rx[z] = gw4_rx[...]
            for i, j in enumerate(zpeers):
                send(gw5_rx.at[z], gw5_rx.at[z], gw_s.at[4, i], gw_r.at[4, z], device(x, y, j, k))

    for n, o in enumerate(ORDER):
        p = group(o)[2]
        if n == 1:
            pass_grads(4, 3, (2, 1))
            pass_grads(2, 5, (1,))
        elif n == 3:
            pass_grads(6, 6, (1,))
            arrived(grad_rx.at[p], grad_s.at[0], grad_r.at[p])
        elif o in (5, 3, 7):
            arrived(grad_rx.at[p], grad_s.at[0], grad_r.at[p])
        grads = grad_rx[p] if o else grad_tx[...]
        for c in range(ZH):
            pair, cols = live_tiles(p, c)
            both = jnp.dot(grads, pair, preferred_element_type=F32)
            for s in range(SLOTS):
                i = c * GROUP * SLOTS + n * SLOTS + s
                chain[i] = both[:, s * TILE:(s + 1) * TILE] + chain[prev_sm[i]]
        if n in (3, 5):
            weight_round((n - 3) // 2)

    def block(c, yy, half):
        return chain[last_sm[c * 2 * NY + yy * 2 + half]]

    def send_half(j):
        yy = yp(j)
        for c in range(ZH):
            sib_tx[yy, c] = block(c, yy, 1 - k).astype(BF16)
        send(sib_tx.at[yy], sib_rx.at[yy], sib_s.at[j % NY], sib_r.at[yy], sibling)

    def both_cores(yy, c):
        return block(c, yy, k) + sib_rx[yy, c].astype(F32)

    def reduce_step(s, target, tx, rx, ssem, rsem, dev):
        arrived(sib_rx.at[target], sib_s.at[0], sib_r.at[target])
        for c in (zothers[2], zothers[1], zothers[3], zh):
            value = both_cores(target, c)
            if s > 0:
                arrived(rx.at[s - 1, c], ssem.at[s - 1, c], rsem.at[s - 1, c])
                value += rx[s - 1, c].astype(F32)
            tx[s, c] = value.astype(BF16)
            send(tx.at[s, c], rx.at[s, c], ssem.at[s, c], rsem.at[s, c], dev)

    for s, halves in enumerate(((4, 3), (-3, 2), (-2, 1), (-1, 0))):
        for j in halves:
            send_half(j)
        reduce_step(s, yp(4 - s), plus_tx, plus_rx, plus_s, plus_r, up)
        if s < 3:
            reduce_step(s, yp(s - 3), minus_tx, minus_rx, minus_s, minus_r, down)
        if s < 2:
            weight_round(s + 2)

    arrived(sib_rx.at[y], sib_s.at[0], sib_r.at[y])
    for i in (2, 1, 3, 0):
        j = zothers[i]
        arrived(plus_rx.at[3, j], plus_s.at[3, j], plus_r.at[3, j])
        arrived(minus_rx.at[2, j], minus_s.at[2, j], minus_r.at[2, j])
        value = both_cores(y, j) + plus_rx[3, j].astype(F32) + minus_rx[2, j].astype(F32)
        zred_tx[i] = value.astype(BF16)
        if i > 0:
            send(zred_tx.at[i], zred_rx.at[zh], zred_s.at[i], zred_r.at[zh], partner(j))

    @pl.when(xl == k)
    def _():
        zred_rx[zh] = zred_tx[0]

    @pl.when(xl != k)
    def _():
        copy(zred_tx.at[0], zred_rx.at[zh], zred_s.at[0], zred_r.at[zh], partner(zh)).start()

    for i, j in enumerate(zpeers):
        arrived(gw5_rx.at[j], gw_s.at[4, i], gw_r.at[4, j])
    scale = 1.0 / 256.0
    for i in range(NZ):
        for j in range(GROUP):
            r0, c0 = i * 32 + (j % 4) * 8, (j // 4) * 128
            gw_ref[r0:r0 + 8, c0:c0 + 128] = gw5_rx[i, j] * scale

    for i in range(1, ZH):
        arrived(zred_rx.at[zothers[i]], zred_s.at[i], zred_r.at[zothers[i]])

    @pl.when(xl != k)
    def _():
        arrived(zred_rx.at[zh], zred_s.at[0], zred_r.at[zh])

    gf_ref[...] = jnp.sum(zred_rx[...].astype(F32), axis=0).T.astype(BF16)

    @pl.when(xl != k)
    def _():
        copy(zred_tx.at[0], zred_rx.at[zh], zred_s.at[0], zred_r.at[zh], partner(zh)).wait_send()
        copy(feat_ref, feats.at[xl, y, zh], agz_s.at[0], agz_r.at[zh], partner(zh)).wait_send()

    for c in sent:
        c.wait_send()


def finish(out_in, gf_in, gw_in, out_ref, gf_ref, gw_ref):
    out_ref[...] = out_in[...]
    gf_ref[...] = gf_in[...]
    gw_ref[...] = gw_in[...]


def body(features, weight, cotangent, tile_values, tile_cols, tile_counts):
    cols = tile_cols.reshape(32, SLOTS).T
    counts = tile_counts.reshape(1, 32)
    tiles = tile_values.reshape(2, ZH, 2, 2, SLOTS, TILE, TILE)
    dma, vmem = pltpu.SemaphoreType.DMA, pltpu.VMEM
    spec = pl.BlockSpec(memory_space=pltpu.VMEM)
    block = (D, TILE)
    results = pl.pallas_call(
        kernel,
        out_shape=(
            jax.ShapeDtypeStruct((TILE, D), BF16),
            jax.ShapeDtypeStruct((TILE, D), BF16),
            jax.ShapeDtypeStruct((D, D), F32),
        ),
        in_specs=[spec] * 5 + [pl.BlockSpec(memory_space=pl.ANY)],
        out_specs=(spec,) * 3,
        scratch_shapes=[
            vmem((GROUP, ZH, SLOTS, TILE, TILE), BF16),
            vmem((8, 128), jnp.int32),
            vmem((GROUP, 8, 128), jnp.int32),
            pltpu.SMEM((GROUP, 8, 128), jnp.int32),
            pltpu.SMEM((TERMS,), jnp.int32),
            pltpu.SMEM((ZH * 2 * NY,), jnp.int32),
            vmem((2, NY, ZH, TILE, D), BF16),
            vmem((GROUP, TILE, D), BF16),
            vmem((2, TILE, D), BF16),
            vmem((GROUP, TILE, D), BF16),
            vmem(block, BF16),
            vmem((GROUP,) + block, BF16),
            vmem((TERMS + 1,) + block, F32),
            vmem((NY, ZH) + block, BF16),
            vmem((NY, ZH) + block, BF16),
            vmem((4, ZH) + block, BF16),
            vmem((4, ZH) + block, BF16),
            vmem((3, ZH) + block, BF16),
            vmem((3, ZH) + block, BF16),
            vmem((ZH,) + block, BF16),
            vmem((ZH,) + block, BF16),
            vmem((NZ, GROUP, 8, 128), F32),
            vmem((NZ, GROUP, 8, 128), F32),
            vmem((GROUP, 8, 128), F32),
            vmem((GROUP, 8, 128), F32),
            vmem((NY, 8, 128), F32),
            vmem((GROUP, 8, 128), F32),
            vmem((NZ, GROUP, 8, 128), F32),
            dma((2,)), dma((2,)),
            dma((GROUP, ZH)), dma((GROUP, ZH)),
            dma((GROUP,)), dma((GROUP,)),
            dma((ZH,)), dma((ZH,)),
            dma((4, ZH)), dma((4, ZH)),
            dma((3, ZH)), dma((3, ZH)),
            dma((NY,)), dma((NY,)),
            dma((GROUP,)), dma((GROUP,)),
            dma((GROUP,)), dma((GROUP,)),
            dma((NY,)), dma((NY,)),
            dma((4, ZH)), dma((4, ZH)),
            dma((3, ZH)), dma((3, ZH)),
            dma((ZH,)), dma((ZH,)),
            dma((5, 8)), dma((5, 8)),
        ],
        compiler_params=pltpu.CompilerParams(
            collective_id=0, has_side_effects=True, vmem_limit_bytes=56 * 1024 * 1024
        ),
    )(features, weight, cotangent, cols, counts, tiles)
    return pl.pallas_call(
        finish,
        out_shape=tuple(jax.ShapeDtypeStruct(r.shape, r.dtype) for r in results),
        in_specs=[spec] * 3,
        out_specs=(spec,) * 3,
        compiler_params=pltpu.CompilerParams(vmem_limit_bytes=63 * 1024 * 1024),
    )(*results)


def solution(mesh):
    return jax.shard_map(
        body,
        mesh=mesh,
        in_specs=(
            P(("section", "rep"), None),
            P(),
            P(("section", "rep"), None),
            P("section", "rep", None, None, None, None),
            P("section", "rep", None, None),
            P("section", "rep", None),
        ),
        out_specs=(P(("section", "rep"), None), P(("section", "rep"), None), P()),
        check_vma=False,
    )
```
